256 devices in a mesh: lat: 16 (over z, x_hi), lon: 16 (over y, x_lo, core).
Axes of the slice: x: 4 (x_hi: 2, x_lo: 2; x = x_hi * 2 + x_lo), y: 4, z: 8, core: 2. Of those that a mesh axis runs over, the one named last changes fastest.
Arguments:
- features: bfloat16 [2, 192, 768, 512], P(None, 'lat', 'lon'), may hold values from -6 to 6
- regions: int32 [192, 768], P('lat', 'lon'), may hold values from 0 to 3, as said below
- qkv_weight: bfloat16 [512, 1536], replicated, may hold values from -0.25 to 0.25
- out_weight: bfloat16 [512, 512], replicated, may hold values from -0.25 to 0.25
- grad_output: bfloat16 [2, 192, 768, 512], P(None, 'lat', 'lon'), may hold values from -6 to 6
Outputs:
- output: bfloat16 [2, 192, 768, 512], P(None, 'lat', 'lon')
- grad_features: bfloat16 [2, 192, 768, 512], P(None, 'lat', 'lon')
- grad_qkv: float32 [512, 1536], P(None, ('lat', 'lon'))
- grad_out: float32 [512, 512], P(None, ('lat', 'lon'))
The draws below stay inside these ranges and needn't reach their ends.
Inputs may be any that keep to these rules, and one draw needn't show every extreme that they name: Within a window, regions takes one value on the rows of the shifted frame that came across the seam of the latitude roll (the last 6 rows of the grid) and one value on all other rows; those two values are drawn per window and may be equal. All windows outside the last strip of windows along latitude hold a single value.
All inputs are finite; a program needn't handle non-finite values.
Results may differ from the reference program's by a relative error of at most 0.0093.
Values may be sent and summed in bfloat16 or wider, within the bound.
No kernel may reach another device: no remote copies, remote signals or barrier semaphores. Data moves between devices by JAX's collectives and lax.ppermute only.
A program may use at most 128 MiB of HBM per device.

```python
import jax
import jax.numpy as jnp
from jax import lax

D = 512
HEADS = 8
HEAD_DIM = 64
LEVELS = 2
WINDOW = 12
SHIFT = 6
NLAT = 192
NLON = 768


def draw_regions(key, part):
    key = jax.random.fold_in(key, 11)
    key_top, key_low = jax.random.split(key)
    win_rows = NLAT // WINDOW
    win_cols = NLON // WINDOW
    labels_top = jax.random.randint(key_top, (win_rows, win_cols), 0, 4).astype(jnp.int32)
    labels_low = jax.random.randint(key_low, (win_cols,), 0, 4).astype(jnp.int32)
    labels_top = labels_top.at[win_rows - 1, 0].set(3)
    labels_low = labels_low.at[0].set(0)
    labels_top = labels_top.at[win_rows - 1, 1].set(0)
    labels_low = labels_low.at[1].set(0)
    grid_top = jnp.repeat(jnp.repeat(labels_top, WINDOW, axis=0), WINDOW, axis=1)
    grid_low = jnp.broadcast_to(jnp.repeat(labels_low, WINDOW)[None, :], (NLAT, NLON))
    row_index = jnp.arange(NLAT, dtype=jnp.int32)[:, None]
    return jnp.where(row_index >= NLAT - SHIFT, grid_low, grid_top).astype(jnp.int32)


def levels(stream_key, extent, cuts, smallest, high):
    factor_of = 1.0
    for axis_at, shards_of in cuts:
        draws = jax.random.uniform(jax.random.fold_in(jax.random.fold_in(stream_key, 6), axis_at), (shards_of,), jnp.float32, smallest / len(cuts), high / len(cuts))
        factor_of = factor_of * jnp.repeat(jnp.exp(draws), extent[axis_at] // shards_of).reshape((-1,) + (1,) * (len(extent) - 1 - axis_at))
    return factor_of


def scatter_about(rng, extent, spread, most, pieces=(), held_as=jnp.bfloat16):
    gain = levels(rng, extent, pieces, -0.22, 0.18) if pieces else 1.0
    result = jax.random.normal(rng, extent, jnp.float32) * spread * gain
    return jnp.minimum(jnp.maximum(result, -most), most).astype(held_as)


def setup_inputs(seed: int = 0) -> dict:
    key_list = jax.random.split(jax.random.key(seed), 6)
    return {
        "features": scatter_about(key_list[0], (LEVELS, NLAT, NLON, D), 1.0, 6.0, ((1, 16), (2, 16))),
        "regions": draw_regions(jax.random.fold_in(key_list[5], 71), 0),
        "qkv_weight": scatter_about(key_list[2], (D, 3 * D), D ** -0.5, 0.25),
        "out_weight": scatter_about(key_list[3], (D, D), D ** -0.5, 0.25),
        "grad_output": scatter_about(key_list[4], (LEVELS, NLAT, NLON, D), 1.0, 6.0, ((1, 16), (2, 16))),
    }


def window_pass(moved, grad_moved, region, qkv_weight, out_weight):
    tokens = moved.shape[0]
    scale = HEAD_DIM ** (-0.5)
    qkv = jnp.dot(moved, qkv_weight, preferred_element_type=jnp.float32).astype(jnp.bfloat16)
    query = qkv[:, :D].reshape(tokens, HEADS, HEAD_DIM).astype(jnp.float32)
    keys = qkv[:, D:2 * D].reshape(tokens, HEADS, HEAD_DIM).astype(jnp.float32)
    values = qkv[:, 2 * D:].reshape(tokens, HEADS, HEAD_DIM).astype(jnp.float32)
    scores = jnp.einsum('qhe,khe->hqk', query, keys) * scale
    same = region[:, None] == region[None, :]
    scores = jnp.where(same[None], scores, -1e+30)
    probs = jax.nn.softmax(scores, axis=-1)
    probs_low = probs.astype(jnp.bfloat16)
    attended = jnp.einsum('hqk,khe->qhe', probs_low.astype(jnp.float32), values).astype(jnp.bfloat16).reshape(tokens, D)
    branch = jnp.dot(attended, out_weight, preferred_element_type=jnp.float32).astype(jnp.bfloat16)
    grad_att = jnp.dot(grad_moved, out_weight.T, preferred_element_type=jnp.float32).astype(jnp.bfloat16)
    grad_wout = jnp.dot(attended.T, grad_moved, preferred_element_type=jnp.float32)
    grad_heads = grad_att.reshape(tokens, HEADS, HEAD_DIM).astype(jnp.float32)
    grad_probs = jnp.einsum('qhe,khe->hqk', grad_heads, values)
    grad_scores = probs * (grad_probs - lax.optimization_barrier(jnp.sum(grad_probs * probs, axis=-1, keepdims=True))) * scale
    grad_scores = grad_scores.astype(jnp.bfloat16).astype(jnp.float32)
    grad_query = jnp.einsum('hqk,khe->qhe', grad_scores, keys).astype(jnp.bfloat16)
    grad_keys = jnp.einsum('hqk,qhe->khe', grad_scores, query).astype(jnp.bfloat16)
    grad_values = jnp.einsum('hqk,qhe->khe', probs_low.astype(jnp.float32), grad_heads).astype(jnp.bfloat16)
    grad_rows = jnp.concatenate([grad_query.reshape(tokens, D), grad_keys.reshape(tokens, D), grad_values.reshape(tokens, D)], axis=1)
    grad_wqkv = jnp.dot(moved.T, grad_rows, preferred_element_type=jnp.float32)
    normalized_gradient = jnp.dot(grad_rows, qkv_weight.T, preferred_element_type=jnp.float32).astype(jnp.bfloat16)
    return (branch, normalized_gradient, grad_wqkv, grad_wout)

def to_windows(grid):
    lev, rows, cols, width = grid.shape
    split = grid.reshape(lev, rows // WINDOW, WINDOW, cols // WINDOW, WINDOW, width)
    return split.transpose(1, 3, 0, 2, 4, 5).reshape(-1, lev * WINDOW * WINDOW, width)

def from_windows(wins, lev, rows, cols):
    width = wins.shape[-1]
    split = wins.reshape(rows // WINDOW, cols // WINDOW, lev, WINDOW, WINDOW, width)
    return split.transpose(2, 0, 3, 1, 4, 5).reshape(lev, rows, cols, width)

def region_windows(regions, lev):
    rows, cols = regions.shape
    split = regions.reshape(rows // WINDOW, WINDOW, cols // WINDOW, WINDOW).transpose(0, 2, 1, 3)
    split = split.reshape(-1, 1, WINDOW * WINDOW)
    return jnp.broadcast_to(split, (split.shape[0], lev, WINDOW * WINDOW)).reshape(split.shape[0], lev * WINDOW * WINDOW)

def reference(features, regions, qkv_weight, out_weight, grad_output):
    lev, rows, cols, width = features.shape
    x32 = features.astype(jnp.float32)
    feature_mean = lax.optimization_barrier(jnp.mean(x32, axis=-1, keepdims=True))
    centered_input = x32 - feature_mean
    inverse_deviation = lax.rsqrt(lax.optimization_barrier(jnp.mean(centered_input * centered_input, axis=-1, keepdims=True)) + 1e-05)
    standardized_input = centered_input * inverse_deviation
    normalized_input = standardized_input.astype(jnp.bfloat16)
    moved = jnp.roll(normalized_input, (-SHIFT, -SHIFT), axis=(1, 2))
    grad_moved = jnp.roll(grad_output, (-SHIFT, -SHIFT), axis=(1, 2))
    win_x = to_windows(moved)
    win_g = to_windows(grad_moved)
    win_r = region_windows(regions, lev)

    def step(carry, item):
        branch, grad_n, grad_wqkv, grad_wout = window_pass(item[0], item[1], item[2], qkv_weight, out_weight)
        return ((carry[0] + grad_wqkv, carry[1] + grad_wout), (branch, grad_n))
    init = (jnp.zeros((width, 3 * width), jnp.float32), jnp.zeros((width, width), jnp.float32))
    sums, outs = lax.scan(step, init, (win_x, win_g, win_r))
    branch = jnp.roll(from_windows(outs[0], lev, rows, cols), (SHIFT, SHIFT), axis=(1, 2))
    normalized_gradient = jnp.roll(from_windows(outs[1], lev, rows, cols), (SHIFT, SHIFT), axis=(1, 2)).astype(jnp.float32)
    output = (x32 + branch.astype(jnp.float32)).astype(jnp.bfloat16)
    layernorm_input_gradient = inverse_deviation * (normalized_gradient - lax.optimization_barrier(jnp.mean(normalized_gradient, axis=-1, keepdims=True)) - standardized_input * lax.optimization_barrier(jnp.mean(normalized_gradient * standardized_input, axis=-1, keepdims=True)))
    grad_features = (grad_output.astype(jnp.float32) + layernorm_input_gradient).astype(jnp.bfloat16)
    return (output, grad_features, sums[0], sums[1])
```

```python
import functools

import jax
import jax.numpy as jnp
import numpy as np
from jax import lax
from jax.experimental import pallas as pl
from jax.experimental.pallas import tpu as pltpu
from jax.sharding import PartitionSpec as P

HEADS = 8
WINDOW = 12
SHIFT = 6
LEV, ROWS, COLS, D = 2, 12, 48, 512
HALF = LEV * SHIFT * COLS
WINS = COLS // WINDOW
TOK = HALF // WINS
WTOK = 2 * TOK
RIM = LEV * SHIFT * SHIFT
RIMP = 80
QUAD = 256
GROUPS = D // QUAD
HPG = 4
HD = 64
LOG2E = 1.4426950408889634
VMEM = 56 * 1024 * 1024
NT = (((1,), (1,)), ((), ()))
TN = (((0,), (0,)), ((), ()))
f32, bf16 = jnp.float32, jnp.bfloat16


def one_hots():
    place = np.zeros((HALF, HALF), np.float32)
    rim = np.zeros((HALF, RIMP), np.float32)
    cut = np.zeros((RIMP, HALF), np.float32)
    for lev in range(LEV):
        for row in range(SHIFT):
            line = lev * SHIFT + row
            for col in range(COLS):
                win, at = divmod(col, WINDOW)
                to = win * TOK + line * WINDOW + at
                if col + SHIFT < COLS:
                    place[to, line * COLS + col + SHIFT] = 1
                else:
                    rim[to, line * SHIFT + col + SHIFT - COLS] = 1
                if col < SHIFT:
                    cut[line * SHIFT + col, line * COLS + col] = 1
    return place, rim, cut


PLACE, RIMS, CUT = one_hots()


def mm(a, b, dims=(((1,), (0,)), ((), ()))):
    return lax.dot_general(a, b, dims, preferred_element_type=f32)


def move(one_hot, x):
    return mm(one_hot, x).astype(bf16)


def ahead_kernel(x_ref, g_ref, cut_ref, n_ref, up_ref, lo_ref):
    for lev in range(LEV):
        x = x_ref[lev].reshape(ROWS * COLS, D).astype(f32)
        c = x - jnp.mean(x, axis=-1, keepdims=True)
        n = c * lax.rsqrt(jnp.mean(c * c, axis=-1, keepdims=True) + 1e-5)
        n_ref[lev] = n.astype(bf16).reshape(ROWS, COLS, D)
    cut = cut_ref[...]
    for at, src in enumerate((n_ref, g_ref)):
        lo_ref[at] = move(cut, src[:, :SHIFT].reshape(HALF, D))
        up_ref[at] = move(cut, src[:, SHIFT:].reshape(HALF, D))


def window_kernel(
    same_ref, n_ref, g_ref, nrow_ref, grow_ref, up_ref, lo_ref, place_ref, rim_ref, rimt_ref,
    wq_ref, wk_ref, wv_ref, wo_ref, wqkv_ref, wout_ref,
    rup_ref, rlo_ref, eup_ref, elo_ref, gw_ref, go_ref,
    x_s, g_s, q_s, k_s, v_s, a_s, s_s, dp_s, p_s, ds_s, qs_s, gs_s, att_s, rows_s,
):
    group = pl.program_id(0)

    @pl.when(group == 0)
    def _():
        for at, (own, row, dst) in enumerate(((n_ref, nrow_ref, x_s), (g_ref, grow_ref, g_s))):
            upper = mm(place_ref[...], own[:, SHIFT:].reshape(HALF, D)) + mm(rim_ref[...], up_ref[at])
            lower = mm(place_ref[...], row[...].reshape(HALF, D)) + mm(rim_ref[...], lo_ref[at])
            for w in range(WINS):
                dst[w * WTOK : w * WTOK + TOK] = upper[w * TOK : (w + 1) * TOK].astype(bf16)
                dst[w * WTOK + TOK : (w + 1) * WTOK] = lower[w * TOK : (w + 1) * TOK].astype(bf16)

    q_s[...] = mm(x_s[...], wq_ref[...]).astype(bf16)
    k_s[...] = mm(x_s[...], wk_ref[...]).astype(bf16)
    v_s[...] = mm(x_s[...], wv_ref[...]).astype(bf16)
    a_s[...] = mm(g_s[...], wo_ref[...], NT).astype(bf16)

    lane = lax.broadcasted_iota(jnp.int32, (1, QUAD), 1)
    head_of = lane // HD
    query = lax.broadcasted_iota(jnp.int32, (1, HPG * WTOK), 1)
    in_upper = lax.rem(query, WTOK) < TOK

    def window(w, carry):
        rows = pl.ds(pl.multiple_of(w * WTOK, WTOK), WTOK)
        same = same_ref[w] != 0
        q, k, v, a = q_s[rows], k_s[rows], v_s[rows], a_s[rows]
        for h in range(HPG):
            qs_s[h * WTOK : (h + 1) * WTOK] = jnp.where(head_of == h, q, jnp.zeros_like(q))
            gs_s[h * WTOK : (h + 1) * WTOK] = jnp.where(head_of == h, a, jnp.zeros_like(a))
        s_s[...] = mm(k, qs_s[...], NT)
        dp_s[...] = mm(v, gs_s[...], NT)
        for j in range(HPG * WTOK // 128):
            cols = slice(128 * j, 128 * (j + 1))
            up = in_upper[:, cols]
            s_up, s_lo = s_s[:TOK, cols], s_s[TOK:, cols]
            m_up = jnp.max(s_up, axis=0, keepdims=True)
            m_lo = jnp.max(s_lo, axis=0, keepdims=True)
            m = jnp.where(same, jnp.maximum(m_up, m_lo), jnp.where(up, m_up, m_lo))
            from_up = jnp.where(jnp.logical_or(same, up), m, 1e30)
            from_lo = jnp.where(jnp.logical_and(jnp.logical_not(same), up), 1e30, m)
            c = LOG2E * HD**-0.5
            e_up = jnp.exp2((s_up - from_up) * c)
            e_lo = jnp.exp2((s_lo - from_lo) * c)
            total = jnp.sum(e_up, axis=0, keepdims=True) + jnp.sum(e_lo, axis=0, keepdims=True)
            p = jnp.concatenate([e_up, e_lo], axis=0) * (1.0 / total)
            p_s[:, cols] = p.astype(bf16)
            dp = dp_s[:, cols]
            delta = jnp.sum(dp * p, axis=0, keepdims=True)
            ds_s[:, cols] = (p * (dp - delta) * HD**-0.5).astype(bf16)
        att = mm(p_s[...], v, TN)
        gq = mm(ds_s[...], k, TN)
        gk = mm(ds_s[...], qs_s[...])
        gv = mm(p_s[...], gs_s[...])

        def pick(stack):
            out = stack[:WTOK]
            for h in range(1, HPG):
                out = jnp.where(head_of == h, stack[h * WTOK : (h + 1) * WTOK], out)
            return out.astype(bf16)

        att_s[group, rows] = pick(att)
        rows_s[group, rows] = pick(gq)
        rows_s[GROUPS + group, rows] = gk.astype(bf16)
        rows_s[2 * GROUPS + group, rows] = gv.astype(bf16)
        return carry

    lax.fori_loop(0, WINS, window, 0)

    gw_ref[0, 0] = mm(rows_s[group], x_s[...], TN)
    gw_ref[1, 0] = mm(rows_s[GROUPS + group], x_s[...], TN)
    gw_ref[2, 0] = mm(rows_s[2 * GROUPS + group], x_s[...], TN)
    go_ref[...] = mm(g_s[...], att_s[group], TN)

    @pl.when(group == GROUPS - 1)
    def _():
        def back(w, carry):
            rows = pl.ds(pl.multiple_of(w * WTOK, WTOK), WTOK)
            to = pl.ds(pl.multiple_of(w * TOK, TOK), TOK)
            branch = sum(mm(att_s[i, rows], wout_ref[QUAD * i : QUAD * (i + 1)]) for i in range(GROUPS))
            gn = sum(
                mm(rows_s[i, rows], wqkv_ref[:, QUAD * i : QUAD * (i + 1)], NT)
                for i in range(3 * GROUPS)
            )
            for at, full in enumerate((branch, gn)):
                rup_ref[at, to] = full[:TOK].astype(bf16)
                rlo_ref[at, to] = full[TOK:].astype(bf16)
            return carry

        lax.fori_loop(0, WINS, back, 0)
        for at in range(2):
            eup_ref[at] = move(rimt_ref[...], rup_ref[at])
            elo_ref[at] = move(rimt_ref[...], rlo_ref[at])


def behind_kernel(
    x_ref, g_ref, rup_ref, rlo_ref, eup_ref, elo_ref, placet_ref, cutt_ref, o_ref, gf_ref
):
    for rows, ret, edge in (
        (slice(0, SHIFT), rlo_ref, elo_ref),
        (slice(SHIFT, ROWS), rup_ref, eup_ref),
    ):
        branch = move(placet_ref[...], ret[0]).astype(f32) + move(cutt_ref[...], edge[0]).astype(f32)
        gn = move(placet_ref[...], ret[1]).astype(f32) + move(cutt_ref[...], edge[1]).astype(f32)
        x = x_ref[:, rows].reshape(HALF, D).astype(f32)
        c = x - jnp.mean(x, axis=-1, keepdims=True)
        rstd = lax.rsqrt(jnp.mean(c * c, axis=-1, keepdims=True) + 1e-5)
        xhat = c * rstd
        o_ref[:, rows] = (x + branch).astype(bf16).reshape(LEV, SHIFT, COLS, D)
        along = jnp.mean(gn * xhat, axis=-1, keepdims=True)
        dx = rstd * (gn - jnp.mean(gn, axis=-1, keepdims=True) - xhat * along)
        g = g_ref[:, rows].reshape(HALF, D).astype(f32)
        gf_ref[:, rows] = (g + dx).astype(bf16).reshape(LEV, SHIFT, COLS, D)


def shift_to(x, by_lat, by_lon):
    rows, cols = lax.axis_size("lat"), lax.axis_size("lon")
    pairs = []
    for i in range(rows):
        for j in range(cols):
            to = ((i + by_lat) % rows) * cols + (j + by_lon) % cols
            pairs.append((i * cols + j, to))
    return lax.ppermute(x, ("lat", "lon"), pairs)


def whole(shape):
    return pl.BlockSpec(shape, lambda *_: (0,) * len(shape))


def params():
    return pltpu.CompilerParams(vmem_limit_bytes=VMEM)


def windows(same, n, g, nrow, grow, up, lo, qkv_weight, out_weight):
    place, rim = jnp.asarray(PLACE, bf16), jnp.asarray(RIMS, bf16)
    half, edge = (2, HALF, D), (2, RIMP, D)
    tokens = WINS * WTOK
    one = pl.Buffered(1)

    def fixed(shape):
        return pl.BlockSpec(shape, lambda *_: (0,) * len(shape), pipeline_mode=one)

    return pl.pallas_call(
        window_kernel,
        grid=(GROUPS,),
        in_specs=[pl.BlockSpec(memory_space=pltpu.SMEM)]
        + [fixed(a.shape) for a in (n, g, nrow, grow, up, lo, place, rim, rim.T)]
        + [
            pl.BlockSpec((D, QUAD), lambda i: (0, i)),
            pl.BlockSpec((D, QUAD), lambda i: (0, GROUPS + i)),
            pl.BlockSpec((D, QUAD), lambda i: (0, 2 * GROUPS + i)),
            pl.BlockSpec((QUAD, D), lambda i: (i, 0)),
            fixed(qkv_weight.shape),
            fixed(out_weight.shape),
        ],
        out_specs=[
            whole(half),
            whole(half),
            whole(edge),
            whole(edge),
            pl.BlockSpec((3, 1, QUAD, D), lambda i: (0, i, 0, 0)),
            pl.BlockSpec((D, QUAD), lambda i: (0, i)),
        ],
        out_shape=[
            jax.ShapeDtypeStruct(half, bf16),
            jax.ShapeDtypeStruct(half, bf16),
            jax.ShapeDtypeStruct(edge, bf16),
            jax.ShapeDtypeStruct(edge, bf16),
            jax.ShapeDtypeStruct((3, GROUPS, QUAD, D), f32),
            jax.ShapeDtypeStruct((D, D), f32),
        ],
        scratch_shapes=[
            pltpu.VMEM((tokens, D), bf16),
            pltpu.VMEM((tokens, D), bf16),
            pltpu.VMEM((tokens, QUAD), bf16),
            pltpu.VMEM((tokens, QUAD), bf16),
            pltpu.VMEM((tokens, QUAD), bf16),
            pltpu.VMEM((tokens, QUAD), bf16),
            pltpu.VMEM((WTOK, HPG * WTOK), f32),
            pltpu.VMEM((WTOK, HPG * WTOK), f32),
            pltpu.VMEM((WTOK, HPG * WTOK), bf16),
            pltpu.VMEM((WTOK, HPG * WTOK), bf16),
            pltpu.VMEM((HPG * WTOK, QUAD), bf16),
            pltpu.VMEM((HPG * WTOK, QUAD), bf16),
            pltpu.VMEM((GROUPS, tokens, QUAD), bf16),
            pltpu.VMEM((3 * GROUPS, tokens, QUAD), bf16),
        ],
        compiler_params=params(),
    )(
        same, n, g, nrow, grow, up, lo, place, rim, rim.T,
        qkv_weight, qkv_weight, qkv_weight, out_weight, qkv_weight, out_weight,
    )


def shards(features, regions, qkv_weight, out_weight, grad_output):
    edge = jax.ShapeDtypeStruct((2, RIMP, D), bf16)
    cut = jnp.asarray(CUT, bf16)
    same = (regions[0, ::WINDOW] == regions[SHIFT, ::WINDOW]).astype(jnp.int32)
    grow = shift_to(grad_output[:, :SHIFT], -1, 0)
    normed, up, lo = pl.pallas_call(
        ahead_kernel,
        out_shape=[jax.ShapeDtypeStruct(features.shape, bf16), edge, edge],
        compiler_params=params(),
    )(features, grad_output, cut)
    nrow = shift_to(normed[:, :SHIFT], -1, 0)
    up = shift_to(up, 0, -1)
    lo = shift_to(lo, -1, -1)
    rup, rlo, eup, elo, gw, go = windows(
        same, normed, grad_output, nrow, grow, up, lo, qkv_weight, out_weight
    )
    rlo = shift_to(rlo, 1, 0)
    eup = shift_to(eup, 0, 1)
    elo = shift_to(elo, 1, 1)
    output, grad_features = pl.pallas_call(
        behind_kernel,
        out_shape=[jax.ShapeDtypeStruct(features.shape, bf16)] * 2,
        compiler_params=params(),
    )(features, grad_output, rup, rlo, eup, elo, jnp.asarray(PLACE.T, bf16), cut.T)

    rows, cols = lax.axis_size("lat"), lax.axis_size("lon")
    both = jnp.concatenate([gw.reshape(rows, cols, -1, D), go.reshape(rows, cols, -1, D)], axis=2)
    part = lax.all_to_all(both.astype(bf16), "lon", 1, 1).astype(f32).sum(1)
    part = lax.all_to_all(part.astype(bf16), "lat", 0, 0).astype(f32).sum(0)
    span = gw.size // D // (rows * cols)
    return (output, grad_features, part[:span].T, part[span:].T)


def solution(mesh):
    return jax.shard_map(
        shards,
        mesh=mesh,
        in_specs=(
            P(None, "lat", "lon", None),
            P("lat", "lon"),
            P(),
            P(),
            P(None, "lat", "lon", None),
        ),
        out_specs=(
            P(None, "lat", "lon", None),
            P(None, "lat", "lon", None),
            P(None, ("lat", "lon")),
            P(None, ("lat", "lon")),
        ),
        check_vma=False,
    )
```

```python
import functools

import jax
import jax.numpy as jnp
import numpy as np
from jax import lax
from jax.experimental import pallas as pl
from jax.experimental.pallas import tpu as pltpu
from jax.sharding import PartitionSpec as P

HEADS = 8
WINDOW = 12
SHIFT = 6
LEV, ROWS, COLS, D = 2, 12, 48, 512
LATS, LONS = 16, 16
HALF = LEV * SHIFT * COLS
WINS = COLS // WINDOW
TOK = HALF // WINS
WTOK = 2 * TOK
RIM = LEV * SHIFT * SHIFT
RIMP = 80
PACKED = HALF - RIM + 8
QUAD = 256
GROUPS = D // QUAD
HPG = 4
HD = 64
CHUNK = 2
CTOK = CHUNK * WTOK
SPLIT = CHUNK * TOK
LOG2E = 1.4426950408889634
VMEM = 60 * 1024 * 1024
NT = (((1,), (1,)), ((), ()))
TN = (((0,), (0,)), ((), ()))
f32, bf16 = jnp.float32, jnp.bfloat16
SPAN = 3 * D // (LATS * LONS)
SPAN_OUT = D // (LATS * LONS)
GW = 3 * QUAD // LONS
GO = SPAN_OUT * LATS // 2


def one_hots():
    place = np.zeros((PACKED, HALF), np.float32)
    cut = np.zeros((RIMP, HALF), np.float32)
    for line in range(LEV * SHIFT):
        for col in range(COLS - SHIFT):
            win, at = divmod(col, WINDOW)
            wide = WINDOW if win < WINS - 1 else SHIFT
            place[win * TOK + line * wide + at, line * COLS + col + SHIFT] = 1
        for col in range(SHIFT):
            cut[line * SHIFT + col, line * COLS + col] = 1
    return place, cut


def orders():
    by_lon = np.zeros((GROUPS, LONS * GW, 3 * QUAD), np.float32)
    out_by_lon = np.zeros((D, D), np.float32)
    by_lat = np.zeros((LONS, LATS * 8, LATS * 8), np.float32)
    for group in range(GROUPS):
        filled = [0] * LONS
        for row in range(3 * QUAD):
            column = row // QUAD * D + group * QUAD + row % QUAD
            device, at = divmod(column, SPAN)
            lat, lon = divmod(device, LONS)
            by_lon[group, lon * GW + filled[lon], row] = 1
            by_lat[lon, lat * 8 + at, group * GW + filled[lon]] = 1
            filled[lon] += 1
        assert filled == [GW] * LONS
    for row in range(D):
        device, at = divmod(row, SPAN_OUT)
        lat, lon = divmod(device, LONS)
        out_by_lon[lon * 2 * GO + lat * SPAN_OUT + at, row] = 1
    for lat in range(LATS):
        for at in range(SPAN_OUT):
            by_lat[:, lat * 8 + SPAN + at, GROUPS * GW + lat * SPAN_OUT + at] = 1
    return by_lon, out_by_lon, by_lat


PLACE, CUT = one_hots()
BY_LON, OUT_BY_LON, BY_LAT = orders()


def mm(a, b, dims=(((1,), (0,)), ((), ()))):
    return lax.dot_general(a, b, dims, preferred_element_type=f32)


def move(one_hot, x):
    return mm(one_hot, x).astype(bf16)


def pack(src, place_ref, cut_ref, outs):
    upa_ref, loa_ref, upb_ref, lob_ref, eup_ref, elo_ref = outs
    for rows, a_ref, b_ref, e_ref in (
        (slice(SHIFT, ROWS), upa_ref, upb_ref, eup_ref),
        (slice(0, SHIFT), loa_ref, lob_ref, elo_ref),
    ):
        half = src[:, rows].reshape(HALF, D)
        a_ref[...] = move(place_ref[:SPLIT], half)
        b_ref[...] = move(place_ref[SPLIT:], half)
        e_ref[...] = move(cut_ref[...], half)


def ahead_kernel(x_ref, g_ref, place_ref, cut_ref, *refs):
    n_s = refs[-1]
    for lev in range(LEV):
        x = x_ref[lev].reshape(ROWS * COLS, D).astype(f32)
        c = x - jnp.mean(x, axis=-1, keepdims=True)
        n = c * lax.rsqrt(jnp.mean(c * c, axis=-1, keepdims=True) + 1e-5)
        n_s[lev] = n.astype(bf16).reshape(ROWS, COLS, D)
    for at, src in enumerate((n_s, g_ref)):
        pack(src, place_ref, cut_ref, [r.at[at] for r in refs[:-1]])


def attend(same_ref, first, x_s, g_s, wq_ref, wk_ref, wv_ref, wo_ref, att_ref, rows_ref, scratch):
    q_s, k_s, v_s, a_s, s_s, dp_s, p_s, ds_s, qs_s, gs_s = scratch
    q_s[...] = mm(x_s[...], wq_ref[...]).astype(bf16)
    k_s[...] = mm(x_s[...], wk_ref[...]).astype(bf16)
    v_s[...] = mm(x_s[...], wv_ref[...]).astype(bf16)
    a_s[...] = mm(g_s[...], wo_ref[...], NT).astype(bf16)

    lane = lax.broadcasted_iota(jnp.int32, (1, QUAD), 1)
    head_of = lane // HD
    query = lax.broadcasted_iota(jnp.int32, (1, HPG * WTOK), 1)
    in_upper = lax.rem(query, WTOK) < TOK

    def window(w, carry):
        rows = pl.ds(pl.multiple_of(w * WTOK, WTOK), WTOK)
        same = same_ref[first + w] != 0
        q, k, v, a = q_s[rows], k_s[rows], v_s[rows], a_s[rows]
        for h in range(HPG):
            qs_s[h * WTOK : (h + 1) * WTOK] = jnp.where(head_of == h, q, jnp.zeros_like(q))
            gs_s[h * WTOK : (h + 1) * WTOK] = jnp.where(head_of == h, a, jnp.zeros_like(a))
        s_s[...] = mm(k, qs_s[...], NT)
        dp_s[...] = mm(v, gs_s[...], NT)
        for j in range(HPG * WTOK // 128):
            cols = slice(128 * j, 128 * (j + 1))
            up = in_upper[:, cols]
            s_up, s_lo = s_s[:TOK, cols], s_s[TOK:, cols]
            m_up = jnp.max(s_up, axis=0, keepdims=True)
            m_lo = jnp.max(s_lo, axis=0, keepdims=True)
            m = jnp.where(same, jnp.maximum(m_up, m_lo), jnp.where(up, m_up, m_lo))
            from_up = jnp.where(jnp.logical_or(same, up), m, 1e30)
            from_lo = jnp.where(jnp.logical_and(jnp.logical_not(same), up), 1e30, m)
            c = LOG2E * HD**-0.5
            e_up = jnp.exp2((s_up - from_up) * c)
            e_lo = jnp.exp2((s_lo - from_lo) * c)
            total = jnp.sum(e_up, axis=0, keepdims=True) + jnp.sum(e_lo, axis=0, keepdims=True)
            p = jnp.concatenate([e_up, e_lo], axis=0) * (1.0 / total)
            p_s[:, cols] = p.astype(bf16)
            dp = dp_s[:, cols]
            delta = jnp.sum(dp * p, axis=0, keepdims=True)
            ds_s[:, cols] = (p * (dp - delta) * HD**-0.5).astype(bf16)
        att = mm(p_s[...], v, TN)
        gq = mm(ds_s[...], k, TN)
        gk = mm(ds_s[...], qs_s[...])
        gv = mm(p_s[...], gs_s[...])

        def pick(stack):
            out = stack[:WTOK]
            for h in range(1, HPG):
                out = jnp.where(head_of == h, stack[h * WTOK : (h + 1) * WTOK], out)
            return out.astype(bf16)

        att_ref[0, rows] = pick(att)
        rows_ref[0, 0, rows] = pick(gq)
        rows_ref[1, 0, rows] = gk.astype(bf16)
        rows_ref[2, 0, rows] = gv.astype(bf16)
        return carry

    lax.fori_loop(0, CHUNK, window, 0)


def gather(rimmed, up_ref, lo_ref, eup_ref, elo_ref, x_ref, g_ref):
    for at, dst in enumerate((x_ref, g_ref)):
        for half, (src, rim) in enumerate(((up_ref, eup_ref), (lo_ref, elo_ref))):
            for w in range(CHUNK):
                if rimmed and w == CHUNK - 1:
                    here = src[at, w * TOK :].astype(f32)[:RIM]
                    there = rim[at].astype(f32)[:RIM]
                    block = jnp.concatenate([here, there], axis=0).astype(bf16)
                else:
                    block = src[at, w * TOK : (w + 1) * TOK]
                dst[w * WTOK + half * TOK : w * WTOK + (half + 1) * TOK] = block


def chunk_a_kernel(same_ref, up_ref, lo_ref, wqkv_ref, wout_ref, *refs):
    wq_ref, wk_ref, wv_ref, wo_ref, x_ref, g_ref, att_ref, rows_ref, rup_ref, rlo_ref = refs[:10]
    att_s, rows_s, *scratch = refs[10:]
    group = pl.program_id(0)

    @pl.when(group == 0)
    def _():
        gather(False, up_ref, lo_ref, None, None, x_ref, g_ref)

    attend(same_ref, 0, x_ref, g_ref, wq_ref, wk_ref, wv_ref, wo_ref, att_ref, rows_ref, scratch)
    att_s[group] = att_ref[0]
    rows_s[group] = rows_ref[:, 0]

    @pl.when(group == GROUPS - 1)
    def _():
        atts = [att_s.at[i] for i in range(GROUPS)]
        rows = [rows_s.at[i] for i in range(GROUPS)]
        back_kernel(False, atts, rows, wqkv_ref, wout_ref, rup_ref, rlo_ref)


def chunk_b_kernel(same_ref, up_ref, lo_ref, eup_ref, elo_ref, *refs):
    *parts, wq_ref, wk_ref, wv_ref, wo_ref, x_ref, g_ref, att_ref, rows_ref, o_ref = refs[:15]
    gather(True, up_ref, lo_ref, eup_ref, elo_ref, x_ref, g_ref)
    attend(
        same_ref, CHUNK, x_ref, g_ref, wq_ref, wk_ref, wv_ref, wo_ref, att_ref, rows_ref, refs[15:]
    )
    reduce_ready(*parts[:4], x_ref, g_ref, att_ref, rows_ref, *parts[4:], o_ref)


def chunk_c_kernel(same_ref, x_ref, g_ref, *refs):
    *parts, wq_ref, wk_ref, wv_ref, wo_ref, att_ref, rows_ref, o_ref = refs[:13]
    attend(
        same_ref, CHUNK, x_ref, g_ref, wq_ref, wk_ref, wv_ref, wo_ref, att_ref, rows_ref, refs[13:]
    )
    reduce_ready(*parts[:4], x_ref, g_ref, att_ref, rows_ref, *parts[4:], o_ref)


def reduce_ready(xa_ref, ga_ref, aa_ref, ra_ref, xb_ref, gb_ref, ab_ref, rb_ref, by_ref, out_by_ref, o_ref):
    parts = []
    for i in range(3):
        total = mm(ra_ref[i, 0], xa_ref[...], TN) + mm(rb_ref[i, 0], xb_ref[...], TN)
        parts.append(total.astype(bf16))
    rows = jnp.concatenate(parts, axis=0)
    o_ref[:, :GW] = move(by_ref[0], rows).reshape(LONS, GW, D)
    out = (mm(ga_ref[...], aa_ref[0], TN) + mm(gb_ref[...], ab_ref[0], TN)).astype(bf16)
    out = move(out_by_ref[...], out).reshape(LONS, 2, GO, QUAD)
    for half in range(2):
        o_ref[:, GW:, QUAD * half : QUAD * (half + 1)] = out[:, half]


def back_kernel(rimmed, att_refs, rows_refs, wqkv_ref, wout_ref, up_ref, lo_ref, *edges):
    for w in range(CHUNK):
        rows = slice(w * WTOK, (w + 1) * WTOK)
        branch = gn = 0.0
        for i in range(GROUPS):
            branch = branch + mm(att_refs[i][rows], wout_ref[QUAD * i : QUAD * (i + 1)])
            for j in range(3):
                at = D * j + QUAD * i
                gn = gn + mm(rows_refs[i][j, rows], wqkv_ref[:, at : at + QUAD], NT)
        for at, full in enumerate((branch, gn)):
            for half, dst in enumerate((up_ref, lo_ref)):
                part = full[half * TOK : (half + 1) * TOK]
                if rimmed and w == CHUNK - 1:
                    pad = jnp.zeros((8, D), f32)
                    dst[at, w * TOK :] = jnp.concatenate([part[:RIM], pad], axis=0).astype(bf16)
                    edges[half][at] = jnp.concatenate([part[RIM:], pad], axis=0).astype(bf16)
                else:
                    dst[at, w * TOK : (w + 1) * TOK] = part.astype(bf16)


def back_b_kernel(a0_ref, r0_ref, a1_ref, r1_ref, wqkv_ref, wout_ref, *outs):
    atts = [a.at[0] for a in (a0_ref, a1_ref)]
    rows = [r.at[:, 0] for r in (r0_ref, r1_ref)]
    back_kernel(True, atts, rows, wqkv_ref, wout_ref, *outs)


def behind_kernel(
    x_ref, g_ref, upa_ref, loa_ref, upb_ref, lob_ref, eup_ref, elo_ref, place_ref, cut_ref,
    o_ref, gf_ref,
):
    for rows, a_ref, b_ref, e_ref in (
        (slice(0, SHIFT), loa_ref, lob_ref, elo_ref),
        (slice(SHIFT, ROWS), upa_ref, upb_ref, eup_ref),
    ):
        both = []
        for at in range(2):
            both.append(
                mm(place_ref[:, :SPLIT], a_ref[at])
                + mm(place_ref[:, SPLIT:], b_ref[at])
                + mm(cut_ref[...], e_ref[at])
            )
        branch, gn = both
        x = x_ref[:, rows].reshape(HALF, D).astype(f32)
        c = x - jnp.mean(x, axis=-1, keepdims=True)
        rstd = lax.rsqrt(jnp.mean(c * c, axis=-1, keepdims=True) + 1e-5)
        xhat = c * rstd
        o_ref[:, rows] = (x + branch).astype(bf16).reshape(LEV, SHIFT, COLS, D)
        along = jnp.mean(gn * xhat, axis=-1, keepdims=True)
        dx = rstd * (gn - jnp.mean(gn, axis=-1, keepdims=True) - xhat * along)
        g = g_ref[:, rows].reshape(HALF, D).astype(f32)
        gf_ref[:, rows] = (g + dx).astype(bf16).reshape(LEV, SHIFT, COLS, D)


def sum_kernel(a_ref, b_ref, by_ref, o_ref):
    rows, outs = [], []
    for ref in (a_ref, b_ref):
        total = ref[0].astype(f32)
        for i in range(1, LONS):
            total = total + ref[i].astype(f32)
        total = total.astype(bf16)
        rows.append(total[:GW])
        outs.append(jnp.concatenate([total[GW:, :QUAD], total[GW:, QUAD:]], axis=0))
    rows.append(jnp.concatenate(outs, axis=1))
    o_ref[...] = move(by_ref[...], jnp.concatenate(rows, axis=0)).reshape(LATS, 8, D)


def send(x, place):
    pairs = []
    for i in range(LATS):
        for j in range(LONS):
            lat, lon = place(i, j)
            pairs.append((i * LONS + j, lat % LATS * LONS + lon % LONS))
    return lax.ppermute(x, ("lat", "lon"), pairs)


def unsend(x, place):
    pairs = []
    for i in range(LATS):
        for j in range(LONS):
            lat, lon = place(i, j)
            pairs.append((lat % LATS * LONS + lon % LONS, i * LONS + j))
    return lax.ppermute(x, ("lat", "lon"), pairs)


def to_upper(i, j):
    return i ^ 1, j


def to_lower(i, j):
    return (i, j) if i % 2 else (i - 2, j)


def to_upper_rim(i, j):
    return i ^ 1, j - 1


def to_lower_rim(i, j):
    return (i, j - 1) if i % 2 else (i - 2, j - 1)


def shaped(*shape, dtype=bf16):
    return jax.ShapeDtypeStruct(shape, dtype)


def call(kernel, us, **kwargs):
    cost = pl.CostEstimate(flops=int(us * 1e9), bytes_accessed=1024, transcendentals=0)
    params = pltpu.CompilerParams(vmem_limit_bytes=VMEM)
    return pl.pallas_call(kernel, cost_estimate=cost, compiler_params=params, **kwargs)


def fixed(shape):
    return pl.BlockSpec(shape, lambda *_: (0,) * len(shape), pipeline_mode=pl.Buffered(1))


def scratches():
    stack = HPG * WTOK
    return [
        *[pltpu.VMEM((CTOK, QUAD), bf16)] * 4,
        *[pltpu.VMEM((WTOK, stack), f32)] * 2,
        *[pltpu.VMEM((WTOK, stack), bf16)] * 2,
        *[pltpu.VMEM((stack, QUAD), bf16)] * 2,
    ]


def weight_specs(group):
    return [
        pl.BlockSpec((D, QUAD), lambda i: (0, group + i)),
        pl.BlockSpec((D, QUAD), lambda i: (0, GROUPS + group + i)),
        pl.BlockSpec((D, QUAD), lambda i: (0, 2 * GROUPS + group + i)),
        pl.BlockSpec((QUAD, D), lambda i: (group + i, 0)),
    ]


def att_spec(group):
    return pl.BlockSpec((1, CTOK, QUAD), lambda i: (group + i, 0, 0))


def rows_spec(group):
    return pl.BlockSpec((3, 1, CTOK, QUAD), lambda i: (0, group + i, 0, 0))


def first_chunk(same, up, lo, qkv_weight, out_weight):
    token = shaped(CTOK, D)
    data = (up, lo, qkv_weight, out_weight)
    outs = [token, token, shaped(GROUPS, CTOK, QUAD), shaped(3, GROUPS, CTOK, QUAD), up, lo]
    return call(
        chunk_a_kernel,
        15,
        grid=(GROUPS,),
        in_specs=[pl.BlockSpec(memory_space=pltpu.SMEM)]
        + [fixed(a.shape) for a in data]
        + weight_specs(0),
        out_specs=[
            fixed(token.shape),
            fixed(token.shape),
            att_spec(0),
            rows_spec(0),
            fixed(up.shape),
            fixed(lo.shape),
        ],
        out_shape=[shaped(*o.shape) for o in outs],
        scratch_shapes=[
            pltpu.VMEM((GROUPS, CTOK, QUAD), bf16),
            pltpu.VMEM((GROUPS, 3, CTOK, QUAD), bf16),
            *scratches(),
        ],
    )(same, *data, qkv_weight, qkv_weight, qkv_weight, out_weight)


def second_chunk(kernel, same, data, before, qkv_weight, out_weight, group, gathers):
    by_lon, out_by_lon = jnp.asarray(BY_LON, bf16), jnp.asarray(OUT_BY_LON, bf16)
    token, ready = shaped(CTOK, D), shaped(LONS, GW + GO, D)
    outs = [shaped(1, CTOK, QUAD), shaped(3, 1, CTOK, QUAD), ready]
    specs = [att_spec(0), rows_spec(0), fixed(ready.shape)]
    if gathers:
        outs = [token, token] + outs
        specs = [fixed(token.shape)] * 2 + specs
    return call(
        kernel,
        11,
        grid=(1,),
        in_specs=[pl.BlockSpec(memory_space=pltpu.SMEM)]
        + [fixed(a.shape) for a in data]
        + [fixed(token.shape)] * 2
        + [att_spec(group), rows_spec(group)]
        + [
            pl.BlockSpec((1, *by_lon.shape[1:]), lambda *_: (group, 0, 0)),
            fixed(out_by_lon.shape),
        ]
        + weight_specs(group),
        out_specs=specs,
        out_shape=outs,
        scratch_shapes=scratches(),
    )(
        same, *data, *before, by_lon, out_by_lon,
        qkv_weight, qkv_weight, qkv_weight, out_weight,
    )


def after(value, *others):
    return lax.optimization_barrier((value, *others))[0]


def shards(features, regions, qkv_weight, out_weight, grad_output):
    place, cut = jnp.asarray(PLACE, bf16), jnp.asarray(CUT, bf16)
    same = (regions[0, ::WINDOW] == regions[SHIFT, ::WINDOW]).astype(jnp.int32)
    same = send(same, to_upper)
    a, b, edge = (2, SPLIT, D), (2, PACKED - SPLIT, D), (2, RIMP, D)
    upa, loa, upb, lob, eup, elo = call(
        ahead_kernel,
        4,
        out_shape=[shaped(*s) for s in (a, a, b, b, edge, edge)],
        scratch_shapes=[pltpu.VMEM((LEV, ROWS, COLS, D), bf16)],
    )(features, grad_output, place, cut)
    upa, loa, same = lax.optimization_barrier((upa, loa, same))
    upa, loa = send(upa, to_upper), send(loa, to_lower)
    upb, lob = send(upb, to_upper), send(lob, to_lower)
    eup, elo = send(eup, to_upper_rim), send(elo, to_lower_rim)
    weights = (qkv_weight, out_weight)

    xa, ga, atta, rowsa, rupa, rloa = first_chunk(same, upa, loa, *weights)
    same, xa, rupa, rloa = lax.optimization_barrier((same, xa, rupa, rloa))
    rupa, rloa = unsend(rupa, to_upper), unsend(rloa, to_lower)
    before = (xa, ga, atta, rowsa)
    xb, gb, attb, rowsb, first = second_chunk(
        chunk_b_kernel, same, (upb, lob, eup, elo), before, *weights, 0, True
    )
    xb, first = lax.optimization_barrier((xb, first))
    first = lax.all_to_all(first, "lon", 0, 0)
    xb, gb, rupa, rloa = lax.optimization_barrier((xb, gb, rupa, rloa))
    attc, rowsc, second = second_chunk(chunk_c_kernel, same, (xb, gb), before, *weights, 1, False)
    attb, second, rowsb = lax.optimization_barrier((attb, second, rowsb))
    second = lax.all_to_all(second, "lon", 0, 0)

    rupb, rlob, reup, relo = call(
        back_b_kernel, 4, out_shape=[shaped(*s) for s in (b, b, edge, edge)]
    )(attb, rowsb, attc, rowsc, *weights)
    rupb, rlob = unsend(rupb, to_upper), unsend(rlob, to_lower)
    reup, relo = unsend(reup, to_upper_rim), unsend(relo, to_lower_rim)
    output, grad_features = call(behind_kernel, 7, out_shape=[shaped(*features.shape)] * 2)(
        features, grad_output, rupa, rloa, rupb, rlob, reup, relo, place.T, cut.T
    )

    by_lat = jnp.asarray(BY_LAT, bf16)[lax.axis_index("lon")]
    part = call(sum_kernel, 2, out_shape=shaped(LATS, 8, D))(first, second, by_lat)
    part = lax.all_to_all(part, "lat", 0, 0).astype(f32).sum(0)
    return (output, grad_features, part[:SPAN].T, part[SPAN:].T)


def solution(mesh):
    return jax.shard_map(
        shards,
        mesh=mesh,
        in_specs=(
            P(None, "lat", "lon", None),
            P("lat", "lon"),
            P(),
            P(),
            P(None, "lat", "lon", None),
        ),
        out_specs=(
            P(None, "lat", "lon", None),
            P(None, "lat", "lon", None),
            P(None, ("lat", "lon")),
            P(None, ("lat", "lon")),
        ),
        check_vma=False,
    )
```

```python
import functools

import jax
import jax.numpy as jnp
import numpy as np
from jax import lax
from jax.experimental import pallas as pl
from jax.experimental.pallas import tpu as pltpu
from jax.sharding import PartitionSpec as P

HEADS = 8
WINDOW = 12
SHIFT = 6
LEV, ROWS, COLS, D = 2, 12, 48, 512
LATS, LONS = 16, 16
HALF = LEV * SHIFT * COLS
WINS = COLS // WINDOW
TOK = HALF // WINS
WTOK = 2 * TOK
RIM = LEV * SHIFT * SHIFT
RIMP = 80
PACKED = HALF - RIM + 8
QUAD = 256
GROUPS = D // QUAD
HPG = 4
HD = 64
CHUNK = 2
CTOK = CHUNK * WTOK
SPLIT = CHUNK * TOK
LOG2E = 1.4426950408889634
VMEM = 60 * 1024 * 1024
NT = (((1,), (1,)), ((), ()))
TN = (((0,), (0,)), ((), ()))
f32, bf16 = jnp.float32, jnp.bfloat16
SPAN = 3 * D // (LATS * LONS)
SPAN_OUT = D // (LATS * LONS)
GW = 3 * QUAD // LONS
GO = SPAN_OUT * LATS
READY = GROUPS * GW + GO
FLAGS = 16


EARLY = 32


def one_hots():
    early = np.zeros((SPLIT, LEV * SHIFT * EARLY), np.float32)
    late = np.zeros((PACKED - SPLIT, HALF), np.float32)
    place = np.zeros((PACKED, HALF), np.float32)
    cut = np.zeros((RIMP, HALF), np.float32)
    for line in range(LEV * SHIFT):
        for col in range(COLS - SHIFT):
            win, at = divmod(col, WINDOW)
            wide = WINDOW if win < WINS - 1 else SHIFT
            to = win * TOK + line * wide + at
            place[to, line * COLS + col + SHIFT] = 1
            if win < CHUNK:
                early[to, line * EARLY + col + SHIFT] = 1
            else:
                late[to - SPLIT, line * COLS + col + SHIFT] = 1
        for col in range(SHIFT):
            cut[line * SHIFT + col, line * COLS + col] = 1
    return early, late, place, cut


def orders():
    by_lon = np.zeros((2, GROUPS, LONS * GW, 3 * QUAD), np.float32)
    out_by_lon = np.zeros((2, D, D), np.float32)
    by_lat = np.zeros((LONS, LATS * 8, LATS * 8), np.float32)

    def place(core, lon):
        return (lon % 2 ^ core) * LONS // 2 + lon // 2

    for group in range(GROUPS):
        filled = [0] * LONS
        for row in range(3 * QUAD):
            column = row // QUAD * D + group * QUAD + row % QUAD
            device, at = divmod(column, SPAN)
            lat, lon = divmod(device, LONS)
            for core in range(2):
                by_lon[core, group, place(core, lon) * GW + filled[lon], row] = 1
            by_lat[lon, lat * 8 + at, group * GW + filled[lon]] = 1
            filled[lon] += 1
        assert filled == [GW] * LONS
    for row in range(D):
        device, at = divmod(row, SPAN_OUT)
        lat, lon = divmod(device, LONS)
        for core in range(2):
            out_by_lon[core, place(core, lon) * GO + lat * SPAN_OUT + at, row] = 1
    for lat in range(LATS):
        for at in range(SPAN_OUT):
            by_lat[:, lat * 8 + SPAN + at, GROUPS * GW + lat * SPAN_OUT + at] = 1
    return by_lon, out_by_lon, by_lat


EARLY_PLACE, LATE_PLACE, PLACE, CUT = one_hots()
BY_LON, OUT_BY_LON, BY_LAT = orders()


def mm(a, b, dims=(((1,), (0,)), ((), ()))):
    return lax.dot_general(a, b, dims, preferred_element_type=f32)


def move(one_hot, x):
    return mm(one_hot, x).astype(bf16)


def normalize(x):
    c = x - jnp.mean(x, axis=-1, keepdims=True)
    return c * lax.rsqrt(jnp.mean(c * c, axis=-1, keepdims=True) + 1e-5)


def early_kernel(x_ref, g_ref, regions_ref, place_ref, up_ref, lo_ref, n_s):
    for lev in range(LEV):
        x = x_ref[lev].reshape(ROWS * EARLY, D).astype(f32)
        n_s[lev] = normalize(x).astype(bf16).reshape(ROWS, EARLY, D)
    for at, src in enumerate((n_s, g_ref)):
        lower = src[:, :SHIFT].reshape(LEV * SHIFT * EARLY, D)
        upper = src[:, SHIFT:].reshape(LEV * SHIFT * EARLY, D)
        up_ref[at, :SPLIT] = move(place_ref[...], upper)
        lo_ref[at] = move(place_ref[...], lower)
        up_ref[at, SPLIT:] = jnp.zeros((FLAGS, D), bf16)
    same = jnp.where(regions_ref[0:1] == regions_ref[SHIFT : SHIFT + 1], 1.0, 0.0)
    row = lax.broadcasted_iota(jnp.int32, (COLS, D), 0)
    lane = lax.broadcasted_iota(jnp.int32, (COLS, D), 1)
    spread = jnp.where(row == lane, 1.0, 0.0).astype(bf16)
    up_ref[0, SPLIT:] = move(jnp.broadcast_to(same, (FLAGS, COLS)).astype(bf16), spread)


def late_kernel(x_ref, g_ref, place_ref, cut_ref, up_ref, lo_ref, eup_ref, elo_ref, n_s):
    for lev in range(LEV):
        x = x_ref[lev].reshape(ROWS * COLS, D).astype(f32)
        n_s[lev] = normalize(x).astype(bf16).reshape(ROWS, COLS, D)
    for at, src in enumerate((n_s, g_ref)):
        for rows, dst, rim in (
            (slice(SHIFT, ROWS), up_ref, eup_ref),
            (slice(0, SHIFT), lo_ref, elo_ref),
        ):
            half = src[:, rows].reshape(HALF, D)
            dst[at] = move(place_ref[...], half)
            rim[at] = move(cut_ref[...], half)


def attend(flags, first, group, x_s, g_s, wqkv_s, wout_s, att_s, rows_s, scratch):
    k_s, v_s, s_s, dp_s, p_s, ds_s, qs_s, gs_s = scratch
    lane = lax.broadcasted_iota(jnp.int32, (1, QUAD), 1)
    head_of = lane // HD
    at = group * QUAD
    wq, wk, wv = (wqkv_s[:, D * i + at : D * i + at + QUAD] for i in range(3))
    wo = wout_s[at : at + QUAD]
    query = lax.broadcasted_iota(jnp.int32, (1, HPG * WTOK), 1)
    in_upper = lax.rem(query, WTOK) < TOK

    def project(w):
        rows = slice(w * WTOK, (w + 1) * WTOK)
        x = x_s[rows]
        k_s[rows] = mm(x, wk).astype(bf16)
        v_s[rows] = mm(x, wv).astype(bf16)
        q = mm(x, wq).astype(bf16)
        a = mm(g_s[rows], wo, NT).astype(bf16)
        for h in range(HPG):
            qs_s[w, h * WTOK : (h + 1) * WTOK] = jnp.where(head_of == h, q, jnp.zeros_like(q))
            gs_s[w, h * WTOK : (h + 1) * WTOK] = jnp.where(head_of == h, a, jnp.zeros_like(a))

    def score(w, cols):
        rows = slice(w * WTOK, (w + 1) * WTOK)
        s_s[w, :, cols] = mm(k_s[rows], qs_s[w, cols], NT)
        dp_s[w, :, cols] = mm(v_s[rows], gs_s[w, cols], NT)

    def soften(w, cols):
        here = lax.broadcasted_iota(jnp.int32, (1, D), 1) == WINDOW * (first + w)
        flag = jnp.sum(jnp.where(here, flags, 0.0), axis=1, keepdims=True)
        same = jnp.broadcast_to(flag, (1, 128)) > 0.5
        up = in_upper[:, cols]
        s_up, s_lo = s_s[w, :TOK, cols], s_s[w, TOK:, cols]
        m_up = jnp.max(s_up, axis=0, keepdims=True)
        m_lo = jnp.max(s_lo, axis=0, keepdims=True)
        m = jnp.where(same, jnp.maximum(m_up, m_lo), jnp.where(up, m_up, m_lo))
        from_up = jnp.where(jnp.logical_or(same, up), m, 1e30)
        from_lo = jnp.where(jnp.logical_and(jnp.logical_not(same), up), 1e30, m)
        c = LOG2E * HD**-0.5
        e_up = jnp.exp2((s_up - from_up) * c)
        e_lo = jnp.exp2((s_lo - from_lo) * c)
        total = jnp.sum(e_up, axis=0, keepdims=True) + jnp.sum(e_lo, axis=0, keepdims=True)
        p = jnp.concatenate([e_up, e_lo], axis=0) * (1.0 / total)
        p_s[w, :, cols] = p.astype(bf16)
        dp = dp_s[w, :, cols]
        delta = jnp.sum(dp * p, axis=0, keepdims=True)
        ds_s[w, :, cols] = (p * ((dp - delta) * HD**-0.5)).astype(bf16)

    def pick(stack):
        out = stack[:WTOK]
        for h in range(1, HPG):
            out = jnp.where(head_of == h, stack[h * WTOK : (h + 1) * WTOK], out)
        return out.astype(bf16)

    def finish(w, part):
        rows = slice(w * WTOK, (w + 1) * WTOK)
        if part == 0:
            att_s[group, rows] = pick(mm(p_s[w], v_s[rows], TN))
        elif part == 1:
            rows_s[group, 0, rows] = pick(mm(ds_s[w], k_s[rows], TN))
        elif part == 2:
            rows_s[group, 1, rows] = mm(ds_s[w], qs_s[w]).astype(bf16)
        else:
            rows_s[group, 2, rows] = mm(p_s[w], gs_s[w]).astype(bf16)

    wide = HPG * WTOK
    tiles = [slice(i, min(i + 256, wide)) for i in range(0, wide, 256)]
    for t in range(CHUNK):
        project(t)
        for tile in tiles:
            score(t, tile)
            for i in range(tile.start, tile.stop, 128):
                soften(t, slice(i, i + 128))
        for j in range(4):
            finish(t, j)


def starts(pairs, sems):
    copies = [pltpu.make_async_copy(src, dst, sems.at[i]) for i, (src, dst) in enumerate(pairs)]
    for copy in copies:
        copy.start()
    return copies


def waits(copies):
    for copy in copies:
        copy.wait()


def whole_windows(up, lo, at, dst, count):
    pairs = []
    for w in range(count):
        for half, src in enumerate((up, lo)):
            to = w * WTOK + half * TOK
            pairs.append((src.at[at, pl.ds(w * TOK, TOK)], dst.at[pl.ds(to, TOK)]))
    return pairs


def chunk_a_kernel(up, lo, wqkv, wout, att, rows, rup, rlo, *refs):
    x_s, g_s, flag_s, wqkv_s, wout_s, att_s, rows_s, rup_s, rlo_s, in_sems, out_sems = refs[:11]
    scratch = refs[11:]
    copies = starts(
        [
            *whole_windows(up, lo, 0, x_s, CHUNK),
            (wqkv, wqkv_s),
            (up.at[0, pl.ds(SPLIT, FLAGS)], flag_s),
            *whole_windows(up, lo, 1, g_s, CHUNK),
            (wout, wout_s),
        ],
        in_sems,
    )
    waits(copies)
    flags = flag_s[...].astype(f32)[0:1]
    outs = []
    for group in range(GROUPS):
        attend(flags, 0, group, x_s, g_s, wqkv_s, wout_s, att_s, rows_s, scratch)
        pairs = [(att_s.at[group], att.at[group]), (rows_s.at[group], rows.at[group])]
        outs += starts(pairs, out_sems.at[pl.ds(2 * group, 2)])
    back(False, att_s, rows_s, wqkv_s, wout_s, rup_s, rlo_s)
    outs += starts([(rup_s, rup), (rlo_s, rlo)], out_sems.at[pl.ds(2 * GROUPS, 2)])
    waits(outs)


def chunk_b_kernel(
    core_ref, upa, loa, up, lo, eup, elo, wqkv, wout, atta, rowsa, by_lon, out_by_lon,
    att, rows, mine, theirs, *refs,
):
    x_s, g_s, flag_s, wqkv_s, wout_s, att_s, rows_s, in_sems, out_sems, late_sems = refs[:10]
    here_s, there_s, xa_s, ga_s, atta_s, rowsa_s, by_s, out_by_s, o_s = refs[10:19]
    scratch = refs[19:]
    core = core_ref[0]
    last = pl.ds((CHUNK - 1) * TOK, RIMP)
    copies = starts(
        [
            *whole_windows(up, lo, 0, x_s, CHUNK - 1),
            *whole_windows(up, lo, 1, g_s, CHUNK - 1),
            (up.at[:, last], here_s.at[0]),
            (lo.at[:, last], here_s.at[1]),
            (eup, there_s.at[0]),
            (elo, there_s.at[1]),
            (wqkv, wqkv_s),
            (wout, wout_s),
            (upa.at[0, pl.ds(SPLIT, FLAGS)], flag_s),
        ],
        in_sems,
    )
    late = starts(
        [
            *whole_windows(upa, loa, 0, xa_s, CHUNK),
            *whole_windows(upa, loa, 1, ga_s, CHUNK),
            (atta, atta_s),
            (rowsa, rowsa_s),
            (by_lon.at[core], by_s),
            (out_by_lon.at[core], out_by_s),
        ],
        late_sems,
    )
    waits(copies)
    for at, dst in enumerate((x_s, g_s)):
        for half in range(2):
            here = here_s[half, at].astype(f32)[:RIM]
            there = there_s[half, at].astype(f32)[:RIM]
            to = (CHUNK - 1) * WTOK + half * TOK
            dst[to : to + TOK] = jnp.concatenate([here, there], axis=0).astype(bf16)
    flags = flag_s[...].astype(f32)[0:1]
    outs = []
    for group in range(GROUPS):
        attend(flags, CHUNK, group, x_s, g_s, wqkv_s, wout_s, att_s, rows_s, scratch)
        pairs = [(att_s.at[group], att.at[group]), (rows_s.at[group], rows.at[group])]
        outs += starts(pairs, out_sems.at[pl.ds(2 * group, 2)])
        if group == 0:
            waits(late)
        parts = []
        for i in range(3):
            total = mm(rowsa_s[group, i], xa_s[...], TN) + mm(rows_s[group, i], x_s[...], TN)
            parts.append(total.astype(bf16))
        ready = move(by_s[group], jnp.concatenate(parts, axis=0))
        o_s[:, :, group * GW : (group + 1) * GW] = ready.reshape(2, LONS // 2, GW, D)
        out = (mm(ga_s[...], atta_s[group], TN) + mm(g_s[...], att_s[group], TN)).astype(bf16)
        out = move(out_by_s[...], out).reshape(2, LONS // 2, GO, QUAD)
        o_s[:, :, GROUPS * GW :, group * QUAD : (group + 1) * QUAD] = out
    outs += starts([(o_s.at[0], mine), (o_s.at[1], theirs)], out_sems.at[pl.ds(2 * GROUPS, 2)])
    waits(outs)


def back(rimmed, att_s, rows_s, wqkv_s, wout_s, up_ref, lo_ref, *edges):
    for w in range(CHUNK):
        rows = slice(w * WTOK, (w + 1) * WTOK)
        branch = gn = 0.0
        for i in range(GROUPS):
            branch = branch + mm(att_s[i, rows], wout_s[QUAD * i : QUAD * (i + 1)])
            for j in range(3):
                at = D * j + QUAD * i
                gn = gn + mm(rows_s[i, j, rows], wqkv_s[:, at : at + QUAD], NT)
        for at, full in enumerate((branch, gn)):
            for half, dst in enumerate((up_ref, lo_ref)):
                part = full[half * TOK : (half + 1) * TOK]
                if rimmed and w == CHUNK - 1:
                    pad = jnp.zeros((8, D), f32)
                    dst[at, w * TOK :] = jnp.concatenate([part[:RIM], pad], axis=0).astype(bf16)
                    edges[half][at] = jnp.concatenate([part[RIM:], pad], axis=0).astype(bf16)
                else:
                    dst[at, w * TOK : (w + 1) * TOK] = part.astype(bf16)


def back_b_kernel(att_ref, rows_ref, wqkv_ref, wout_ref, *outs):
    back(True, att_ref, rows_ref, wqkv_ref, wout_ref, *outs)


def behind_kernel(
    x_ref, g_ref, upa_ref, loa_ref, upb_ref, lob_ref, eup_ref, elo_ref, place_ref, cut_ref,
    o_ref, gf_ref,
):
    def finish(a_ref, b_ref, e_ref):
        both = []
        for at in range(2):
            both.append(
                mm(place_ref[:, :SPLIT], a_ref[at])
                + mm(place_ref[:, SPLIT:], b_ref[at])
                + mm(cut_ref[...], e_ref[at])
            )
        branch, gn = both
        x = x_ref[...].reshape(HALF, D).astype(f32)
        c = x - jnp.mean(x, axis=-1, keepdims=True)
        rstd = lax.rsqrt(jnp.mean(c * c, axis=-1, keepdims=True) + 1e-5)
        xhat = c * rstd
        o_ref[...] = (x + branch).astype(bf16).reshape(LEV, SHIFT, COLS, D)
        along = jnp.mean(gn * xhat, axis=-1, keepdims=True)
        dx = rstd * (gn - jnp.mean(gn, axis=-1, keepdims=True) - xhat * along)
        g = g_ref[...].reshape(HALF, D).astype(f32)
        gf_ref[...] = (g + dx).astype(bf16).reshape(LEV, SHIFT, COLS, D)

    @pl.when(pl.program_id(0) == 0)
    def _():
        finish(loa_ref, lob_ref, elo_ref)

    @pl.when(pl.program_id(0) == 1)
    def _():
        finish(upa_ref, upb_ref, eup_ref)


def sum_kernel(parts_ref, by_ref, o_ref):
    total = parts_ref[0].astype(f32)
    for i in range(1, LONS // 2):
        total = total + parts_ref[i].astype(f32)
    o_ref[...] = move(by_ref[...], total.astype(bf16)).reshape(LATS, 8, D)


def send(x, place):
    pairs = []
    for i in range(LATS):
        for j in range(LONS):
            lat, lon = place(i, j)
            pairs.append((i * LONS + j, lat % LATS * LONS + lon % LONS))
    return lax.ppermute(x, ("lat", "lon"), pairs)


def unsend(x, place):
    pairs = []
    for i in range(LATS):
        for j in range(LONS):
            lat, lon = place(i, j)
            pairs.append((lat % LATS * LONS + lon % LONS, i * LONS + j))
    return lax.ppermute(x, ("lat", "lon"), pairs)


def to_upper(i, j):
    return i ^ 1, j


def to_lower(i, j):
    return (i, j) if i % 2 else (i - 2, j)


def to_upper_rim(i, j):
    return i ^ 1, j - 1


def to_lower_rim(i, j):
    return (i, j - 1) if i % 2 else (i - 2, j - 1)


def shaped(*shape, dtype=bf16):
    return jax.ShapeDtypeStruct(shape, dtype)


def call(kernel, us, **kwargs):
    cost = pl.CostEstimate(flops=int(us * 1e9), bytes_accessed=1024, transcendentals=0)
    params = pltpu.CompilerParams(vmem_limit_bytes=VMEM)
    return pl.pallas_call(kernel, cost_estimate=cost, compiler_params=params, **kwargs)


def whole(shape):
    return pl.BlockSpec(shape, lambda *_: (0,) * len(shape))


def fixed(shape):
    return pl.BlockSpec(shape, lambda *_: (0,) * len(shape), pipeline_mode=pl.Buffered(1))


def anywhere(count):
    return [pl.BlockSpec(memory_space=pl.ANY)] * count


def scratches():
    stack = HPG * WTOK
    return [
        *[pltpu.VMEM((CTOK, QUAD), bf16)] * 2,
        *[pltpu.VMEM((CHUNK, WTOK, stack), f32)] * 2,
        *[pltpu.VMEM((CHUNK, WTOK, stack), bf16)] * 2,
        *[pltpu.VMEM((CHUNK, stack, QUAD), bf16)] * 2,
    ]


def common():
    return [
        pltpu.VMEM((CTOK, D), bf16),
        pltpu.VMEM((CTOK, D), bf16),
        pltpu.VMEM((FLAGS, D), bf16),
        pltpu.VMEM((D, 3 * D), bf16),
        pltpu.VMEM((D, D), bf16),
        pltpu.VMEM((GROUPS, CTOK, QUAD), bf16),
        pltpu.VMEM((GROUPS, 3, CTOK, QUAD), bf16),
    ]


ATT, ROWSET = (GROUPS, CTOK, QUAD), (GROUPS, 3, CTOK, QUAD)


def first_chunk(up, lo, qkv_weight, out_weight):
    ret = (2, SPLIT, D)
    return call(
        chunk_a_kernel,
        13,
        in_specs=anywhere(4),
        out_specs=anywhere(4),
        out_shape=[shaped(*o) for o in (ATT, ROWSET, ret, ret)],
        scratch_shapes=[
            *common(),
            pltpu.VMEM(ret, bf16),
            pltpu.VMEM(ret, bf16),
            pltpu.SemaphoreType.DMA((4 * CHUNK + 3,)),
            pltpu.SemaphoreType.DMA((2 * GROUPS + 2,)),
            *scratches(),
        ],
    )(up, lo, qkv_weight, out_weight)


def second_chunk(core, upa, loa, up, lo, eup, elo, qkv_weight, out_weight, att, rows):
    by_lon, out_by_lon = jnp.asarray(BY_LON, bf16), jnp.asarray(OUT_BY_LON, bf16)
    ready = (LONS // 2, READY, D)
    return call(
        chunk_b_kernel,
        18,
        in_specs=[pl.BlockSpec(memory_space=pltpu.SMEM)] + anywhere(12),
        out_specs=anywhere(4),
        out_shape=[shaped(*o) for o in (ATT, ROWSET, ready, ready)],
        scratch_shapes=[
            *common(),
            pltpu.SemaphoreType.DMA((4 * (CHUNK - 1) + 7,)),
            pltpu.SemaphoreType.DMA((2 * GROUPS + 2,)),
            pltpu.SemaphoreType.DMA((4 * CHUNK + 4,)),
            pltpu.VMEM((2, 2, RIMP, D), bf16),
            pltpu.VMEM((2, 2, RIMP, D), bf16),
            pltpu.VMEM((CTOK, D), bf16),
            pltpu.VMEM((CTOK, D), bf16),
            pltpu.VMEM(ATT, bf16),
            pltpu.VMEM(ROWSET, bf16),
            pltpu.VMEM(by_lon.shape[1:], bf16),
            pltpu.VMEM(out_by_lon.shape[1:], bf16),
            pltpu.VMEM((2, *ready), bf16),
            *scratches(),
        ],
    )(core, upa, loa, up, lo, eup, elo, qkv_weight, out_weight, att, rows, by_lon, out_by_lon)


def other_core(i, j):
    return i, j ^ 1


def shards(features, regions, qkv_weight, out_weight, grad_output):
    place, cut = jnp.asarray(PLACE, bf16), jnp.asarray(CUT, bf16)
    core = (lax.axis_index("lon") % 2).reshape(1)
    a, b, edge = (2, SPLIT, D), (2, PACKED - SPLIT, D), (2, RIMP, D)
    early = pl.BlockSpec((LEV, ROWS, EARLY, D), lambda i: (0, 0, 0, 0))
    up_shape = (2, SPLIT + FLAGS, D)
    upa, loa = call(
        early_kernel,
        3,
        grid=(1,),
        in_specs=[early, early, whole(regions.shape), whole(EARLY_PLACE.shape)],
        out_specs=[whole(up_shape), whole(a)],
        out_shape=[shaped(*up_shape), shaped(*a)],
        scratch_shapes=[pltpu.VMEM((LEV, ROWS, EARLY, D), bf16)],
    )(features, grad_output, regions, jnp.asarray(EARLY_PLACE, bf16))
    features, grad_output, upa, loa = lax.optimization_barrier((features, grad_output, upa, loa))
    upa, loa = send(upa, to_upper), send(loa, to_lower)
    upb, lob, eup, elo = call(
        late_kernel,
        5,
        out_shape=[shaped(*s) for s in (b, b, edge, edge)],
        scratch_shapes=[pltpu.VMEM((LEV, ROWS, COLS, D), bf16)],
    )(features, grad_output, jnp.asarray(LATE_PLACE, bf16), cut)
    upb, lob = send(upb, to_upper), send(lob, to_lower)
    eup, elo = send(eup, to_upper_rim), send(elo, to_lower_rim)
    weights = (qkv_weight, out_weight)

    atta, rowsa, rupa, rloa = first_chunk(upa, loa, *weights)
    atta, rupa, rloa = lax.optimization_barrier((atta, rupa, rloa))
    rupa, rloa = unsend(rupa, to_upper), unsend(rloa, to_lower)
    attb, rowsb, mine, theirs = second_chunk(
        core, upa, loa, upb, lob, eup, elo, *weights, atta, rowsa
    )
    attb, mine, theirs, rupa, rloa = lax.optimization_barrier((attb, mine, theirs, rupa, rloa))
    theirs = send(theirs, other_core)

    rupb, rlob, reup, relo = call(
        back_b_kernel, 4, out_shape=[shaped(*s) for s in (b, b, edge, edge)]
    )(attb, rowsb, *weights)
    ready = (mine.astype(f32) + theirs.astype(f32)).astype(bf16)
    ready, rupb, rlob, reup, relo = lax.optimization_barrier((ready, rupb, rlob, reup, relo))
    cores = [list(range(i, LONS, 2)) for i in range(2)]
    parts = lax.all_to_all(ready, "lon", 0, 0, axis_index_groups=cores)
    rupb, rlob = unsend(rupb, to_upper), unsend(rlob, to_lower)
    reup, relo = unsend(reup, to_upper_rim), unsend(relo, to_lower_rim)
    half = pl.BlockSpec((LEV, SHIFT, COLS, D), lambda i: (0, i, 0, 0))
    returned = (rupa, rloa, rupb, rlob, reup, relo, place.T, cut.T)
    output, grad_features = call(
        behind_kernel,
        6,
        grid=(2,),
        in_specs=[half, half] + [fixed(r.shape) for r in returned],
        out_specs=[half, half],
        out_shape=[shaped(*features.shape)] * 2,
    )(features, grad_output, *returned)

    by_lat = jnp.asarray(BY_LAT, bf16)[lax.axis_index("lon")]
    part = call(sum_kernel, 2, out_shape=shaped(LATS, 8, D))(parts, by_lat)
    part = lax.all_to_all(part, "lat", 0, 0).astype(f32).sum(0)
    return (output, grad_features, part[:SPAN].T, part[SPAN:].T)


def solution(mesh):
    return jax.shard_map(
        shards,
        mesh=mesh,
        in_specs=(
            P(None, "lat", "lon", None),
            P("lat", "lon"),
            P(),
            P(),
            P(None, "lat", "lon", None),
        ),
        out_specs=(
            P(None, "lat", "lon", None),
            P(None, "lat", "lon", None),
            P(None, ("lat", "lon")),
            P(None, ("lat", "lon")),
        ),
        check_vma=False,
    )
```

```python
import functools

import jax
import jax.numpy as jnp
import numpy as np
from jax import lax
from jax.experimental import pallas as pl
from jax.experimental.pallas import tpu as pltpu
from jax.sharding import PartitionSpec as P

HEADS = 8
WINDOW = 12
SHIFT = 6
LEV, ROWS, COLS, D = 2, 12, 48, 512
LATS, LONS = 16, 16
HALF = LEV * SHIFT * COLS
WINS = COLS // WINDOW
TOK = HALF // WINS
WTOK = 2 * TOK
RIM = LEV * SHIFT * SHIFT
RIMP = 80
PACKED = HALF - RIM + 8
QUAD = 256
GROUPS = D // QUAD
HPG = 4
HD = 64
CHUNK = 2
CTOK = CHUNK * WTOK
SPLIT = CHUNK * TOK
LOG2E = 1.4426950408889634
VMEM = 60 * 1024 * 1024
MOST = 63 * 1024 * 1024 + 512 * 1024
NT = (((1,), (1,)), ((), ()))
TN = (((0,), (0,)), ((), ()))
f32, bf16 = jnp.float32, jnp.bfloat16
SPAN = 3 * D // (LATS * LONS)
SPAN_OUT = D // (LATS * LONS)
GW = 3 * QUAD // LONS
GO = SPAN_OUT * LATS
READY = GROUPS * GW + GO
FLAGS = 16


EARLY = 32


def one_hots():
    early = np.zeros((SPLIT, LEV * SHIFT * EARLY), np.float32)
    late = np.zeros((PACKED - SPLIT, HALF), np.float32)
    place = np.zeros((PACKED, HALF), np.float32)
    cut = np.zeros((RIMP, HALF), np.float32)
    for line in range(LEV * SHIFT):
        for col in range(COLS - SHIFT):
            win, at = divmod(col, WINDOW)
            wide = WINDOW if win < WINS - 1 else SHIFT
            to = win * TOK + line * wide + at
            place[to, line * COLS + col + SHIFT] = 1
            if win < CHUNK:
                early[to, line * EARLY + col + SHIFT] = 1
            else:
                late[to - SPLIT, line * COLS + col + SHIFT] = 1
        for col in range(SHIFT):
            cut[line * SHIFT + col, line * COLS + col] = 1
    return early, late, place, cut


def split(lat, lon):
    core, y, last = lon % 2, lon // 4, lat // 2 % 2
    within = (lat // 4 * 2 + lat % 2) * 2 + lon // 2 % 2
    return core, last * 4 + y, within


def orders():
    by_class = np.zeros((2, GROUPS, LONS * GW, 3 * QUAD), np.float32)
    out_by_class = np.zeros((2, D, D), np.float32)
    by_place = np.zeros((LONS, LATS * 8, LATS * 8), np.float32)
    for group in range(GROUPS):
        filled = np.zeros((2, LONS // 2), np.int64)
        for row in range(3 * QUAD):
            column = row // QUAD * D + group * QUAD + row % QUAD
            device, at = divmod(column, SPAN)
            core, rest, within = split(*divmod(device, LONS))
            slot = filled[core, rest]
            for mine in range(2):
                to = ((core ^ mine) * LONS // 2 + rest) * GW + slot
                by_class[mine, group, to, row] = 1
            by_place[core * LONS // 2 + rest, within * 8 + at, group * GW + slot] = 1
            filled[core, rest] += 1
        assert (filled == GW).all()
    for row in range(D):
        device, at = divmod(row, SPAN_OUT)
        core, rest, within = split(*divmod(device, LONS))
        slot = within * SPAN_OUT + at
        for mine in range(2):
            out_by_class[mine, ((core ^ mine) * LONS // 2 + rest) * GO + slot, row] = 1
        by_place[core * LONS // 2 + rest, within * 8 + SPAN + at, GROUPS * GW + slot] = 1
    return by_class, out_by_class, by_place


EARLY_PLACE, LATE_PLACE, PLACE, CUT = one_hots()
BY_LON, OUT_BY_LON, BY_LAT = orders()


def mm(a, b, dims=(((1,), (0,)), ((), ()))):
    return lax.dot_general(a, b, dims, preferred_element_type=f32)


def move(one_hot, x):
    return mm(one_hot, x).astype(bf16)


def normalize(x):
    c = x - jnp.mean(x, axis=-1, keepdims=True)
    return c * lax.rsqrt(jnp.mean(c * c, axis=-1, keepdims=True) + 1e-5)


def early_kernel(x_ref, g_ref, regions_ref, place_ref, up_ref, lo_ref, n_s):
    for lev in range(LEV):
        x = x_ref[lev].reshape(ROWS * EARLY, D).astype(f32)
        n_s[lev] = normalize(x).astype(bf16).reshape(ROWS, EARLY, D)
    for at, src in enumerate((n_s, g_ref)):
        lower = src[:, :SHIFT].reshape(LEV * SHIFT * EARLY, D)
        upper = src[:, SHIFT:].reshape(LEV * SHIFT * EARLY, D)
        up_ref[at, :SPLIT] = move(place_ref[...], upper)
        lo_ref[at] = move(place_ref[...], lower)
        up_ref[at, SPLIT:] = jnp.zeros((FLAGS, D), bf16)
    same = jnp.where(regions_ref[0:1] == regions_ref[SHIFT : SHIFT + 1], 1.0, 0.0)
    row = lax.broadcasted_iota(jnp.int32, (COLS, D), 0)
    lane = lax.broadcasted_iota(jnp.int32, (COLS, D), 1)
    spread = jnp.where(row == lane, 1.0, 0.0).astype(bf16)
    up_ref[0, SPLIT:] = move(jnp.broadcast_to(same, (FLAGS, COLS)).astype(bf16), spread)


def late_kernel(x_ref, g_ref, place_ref, cut_ref, up_ref, lo_ref, eup_ref, elo_ref, n_s):
    for lev in range(LEV):
        x = x_ref[lev].reshape(ROWS * COLS, D).astype(f32)
        n_s[lev] = normalize(x).astype(bf16).reshape(ROWS, COLS, D)
    for at, src in enumerate((n_s, g_ref)):
        for rows, dst, rim in (
            (slice(SHIFT, ROWS), up_ref, eup_ref),
            (slice(0, SHIFT), lo_ref, elo_ref),
        ):
            half = src[:, rows].reshape(HALF, D)
            dst[at] = move(place_ref[...], half)
            rim[at] = move(cut_ref[...], half)


def attend(flags, first, group, x_s, g_s, wqkv_s, wout_s, att_s, rows_s, scratch):
    k_s, v_s, s_s, dp_s, p_s, ds_s, qs_s, gs_s = scratch
    lane = lax.broadcasted_iota(jnp.int32, (1, QUAD), 1)
    head_of = lane // HD
    at = group * QUAD
    wq, wk, wv = (wqkv_s[:, D * i + at : D * i + at + QUAD] for i in range(3))
    wo = wout_s[at : at + QUAD]
    query = lax.broadcasted_iota(jnp.int32, (1, HPG * WTOK), 1)
    in_upper = lax.rem(query, WTOK) < TOK

    def project(w):
        rows = slice(w * WTOK, (w + 1) * WTOK)
        x = x_s[rows]
        k_s[rows] = mm(x, wk).astype(bf16)
        v_s[rows] = mm(x, wv).astype(bf16)
        q = mm(x, wq).astype(bf16)
        a = mm(g_s[rows], wo, NT).astype(bf16)
        for h in range(HPG):
            qs_s[w, h * WTOK : (h + 1) * WTOK] = jnp.where(head_of == h, q, jnp.zeros_like(q))
            gs_s[w, h * WTOK : (h + 1) * WTOK] = jnp.where(head_of == h, a, jnp.zeros_like(a))

    def score(w, cols):
        rows = slice(w * WTOK, (w + 1) * WTOK)
        s_s[w, :, cols] = mm(k_s[rows], qs_s[w, cols], NT)
        dp_s[w, :, cols] = mm(v_s[rows], gs_s[w, cols], NT)

    def soften(w, cols):
        here = lax.broadcasted_iota(jnp.int32, (1, D), 1) == WINDOW * (first + w)
        flag = jnp.sum(jnp.where(here, flags, 0.0), axis=1, keepdims=True)
        same = jnp.broadcast_to(flag, (1, 128)) > 0.5
        up = in_upper[:, cols]
        s_up, s_lo = s_s[w, :TOK, cols], s_s[w, TOK:, cols]
        m_up = jnp.max(s_up, axis=0, keepdims=True)
        m_lo = jnp.max(s_lo, axis=0, keepdims=True)
        m = jnp.where(same, jnp.maximum(m_up, m_lo), jnp.where(up, m_up, m_lo))
        from_up = jnp.where(jnp.logical_or(same, up), m, 1e30)
        from_lo = jnp.where(jnp.logical_and(jnp.logical_not(same), up), 1e30, m)
        c = LOG2E * HD**-0.5
        e_up = jnp.exp2((s_up - from_up) * c)
        e_lo = jnp.exp2((s_lo - from_lo) * c)
        total = jnp.sum(e_up, axis=0, keepdims=True) + jnp.sum(e_lo, axis=0, keepdims=True)
        p = jnp.concatenate([e_up, e_lo], axis=0) * (1.0 / total)
        p_s[w, :, cols] = p.astype(bf16)
        dp = dp_s[w, :, cols]
        delta = jnp.sum(dp * p, axis=0, keepdims=True)
        ds_s[w, :, cols] = (p * ((dp - delta) * HD**-0.5)).astype(bf16)

    def pick(stack):
        out = stack[:WTOK]
        for h in range(1, HPG):
            out = jnp.where(head_of == h, stack[h * WTOK : (h + 1) * WTOK], out)
        return out.astype(bf16)

    def finish(w, part):
        rows = slice(w * WTOK, (w + 1) * WTOK)
        if part == 0:
            att_s[group, rows] = pick(mm(p_s[w], v_s[rows], TN))
        elif part == 1:
            rows_s[group, rows, 0:256] = pick(mm(ds_s[w], k_s[rows], TN))
        elif part == 2:
            rows_s[group, rows, 256:512] = mm(ds_s[w], qs_s[w]).astype(bf16)
        else:
            rows_s[group, rows, 512:768] = mm(p_s[w], gs_s[w]).astype(bf16)

    wide = HPG * WTOK
    tiles = [slice(i, min(i + 256, wide)) for i in range(0, wide, 256)]
    for t in range(CHUNK):
        project(t)
        for tile in tiles:
            score(t, tile)
            for i in range(tile.start, tile.stop, 128):
                soften(t, slice(i, i + 128))
        for j in range(4):
            finish(t, j)


def starts(pairs, sems):
    copies = [pltpu.make_async_copy(src, dst, sems.at[i]) for i, (src, dst) in enumerate(pairs)]
    for copy in copies:
        copy.start()
    return copies


def waits(copies):
    for copy in copies:
        copy.wait()


def whole_windows(up, lo, at, dst, count):
    pairs = []
    for w in range(count):
        for half, src in enumerate((up, lo)):
            to = w * WTOK + half * TOK
            pairs.append((src.at[at, pl.ds(w * TOK, TOK)], dst.at[pl.ds(to, TOK)]))
    return pairs


def chunk_a_kernel(up, lo, wqkv, wout, att, rows, rup, rlo, *refs):
    x_s, g_s, flag_s, wqkv_s, wout_s, att_s, rows_s, rup_s, rlo_s, in_sems, out_sems = refs[:11]
    scratch = refs[11:]
    copies = starts(
        [
            *whole_windows(up, lo, 0, x_s, CHUNK),
            (wqkv, wqkv_s),
            (up.at[0, pl.ds(SPLIT, FLAGS)], flag_s),
            *whole_windows(up, lo, 1, g_s, CHUNK),
            (wout, wout_s),
        ],
        in_sems,
    )
    waits(copies)
    flags = flag_s[...].astype(f32)[0:1]
    outs = []
    for group in range(GROUPS):
        attend(flags, 0, group, x_s, g_s, wqkv_s, wout_s, att_s, rows_s, scratch)
        pairs = [(att_s.at[group], att.at[group]), (rows_s.at[group], rows.at[group])]
        outs += starts(pairs, out_sems.at[pl.ds(2 * group, 2)])
    back(False, att_s, rows_s, wqkv_s, wout_s, rup_s, rlo_s)
    outs += starts([(rup_s, rup), (rlo_s, rlo)], out_sems.at[pl.ds(2 * GROUPS, 2)])
    waits(outs)


def chunk_b_kernel(
    core_ref, upa, loa, up, lo, eup, elo, wqkv, wout, atta, rowsa, by_lon, out_by_lon,
    mine, theirs, rup, rlo, reup, relo, *refs,
):
    x_s, g_s, flag_s, wqkv_s, wout_s, att_s, rows_s, in_sems, out_sems, late_sems = refs[:10]
    here_s, there_s, xa_s, ga_s, atta_s, rowsa_s, by_s, out_by_s, o_s, rup_s, rlo_s, reup_s, relo_s = refs[10:23]
    scratch = refs[23:]
    core = core_ref[0]
    last = pl.ds((CHUNK - 1) * TOK, RIMP)
    copies = starts(
        [
            *whole_windows(up, lo, 0, x_s, CHUNK - 1),
            *whole_windows(up, lo, 1, g_s, CHUNK - 1),
            (up.at[:, last], here_s.at[0]),
            (lo.at[:, last], here_s.at[1]),
            (eup, there_s.at[0]),
            (elo, there_s.at[1]),
            (wqkv, wqkv_s),
            (wout, wout_s),
            (upa.at[0, pl.ds(SPLIT, FLAGS)], flag_s),
        ],
        in_sems,
    )
    late = starts(
        [
            *whole_windows(upa, loa, 0, xa_s, CHUNK),
            *whole_windows(upa, loa, 1, ga_s, CHUNK),
            (atta, atta_s),
            (rowsa, rowsa_s),
            (by_lon.at[core], by_s),
            (out_by_lon.at[core], out_by_s),
        ],
        late_sems,
    )
    waits(copies)
    for at, dst in enumerate((x_s, g_s)):
        for half in range(2):
            here = here_s[half, at].astype(f32)[:RIM]
            there = there_s[half, at].astype(f32)[:RIM]
            to = (CHUNK - 1) * WTOK + half * TOK
            dst[to : to + TOK] = jnp.concatenate([here, there], axis=0).astype(bf16)
    flags = flag_s[...].astype(f32)[0:1]
    for group in range(GROUPS):
        attend(flags, CHUNK, group, x_s, g_s, wqkv_s, wout_s, att_s, rows_s, scratch)
        if group == 0:
            waits(late)
        total = mm(xa_s[...], rowsa_s[group], TN) + mm(x_s[...], rows_s[group], TN)
        ready = mm(by_s[group], total.astype(bf16), NT).astype(bf16)
        o_s[:, :, group * GW : (group + 1) * GW] = ready.reshape(2, LONS // 2, GW, D)
        out = (mm(atta_s[group], ga_s[...], TN) + mm(att_s[group], g_s[...], TN)).astype(bf16)
        out = mm(out_by_s[...], out, NT).astype(bf16).reshape(2, LONS // 2, GO, QUAD)
        o_s[:, :, GROUPS * GW :, group * QUAD : (group + 1) * QUAD] = out
    outs = starts([(o_s.at[0], mine), (o_s.at[1], theirs)], out_sems.at[pl.ds(0, 2)])
    back(True, att_s, rows_s, wqkv_s, wout_s, rup_s, rlo_s, reup_s, relo_s)
    pairs = [(rup_s, rup), (rlo_s, rlo), (reup_s, reup), (relo_s, relo)]
    outs += starts(pairs, out_sems.at[pl.ds(2, 4)])
    waits(outs)


def back(rimmed, att_s, rows_s, wqkv_s, wout_s, up_ref, lo_ref, *edges):
    for w in range(CHUNK):
        rows = slice(w * WTOK, (w + 1) * WTOK)
        branch = gn = 0.0
        for i in range(GROUPS):
            branch = branch + mm(att_s[i, rows], wout_s[QUAD * i : QUAD * (i + 1)])
            for j in range(3):
                at = D * j + QUAD * i
                gn = gn + mm(rows_s[i, rows, QUAD * j : QUAD * (j + 1)], wqkv_s[:, at : at + QUAD], NT)
        for at, full in enumerate((branch, gn)):
            for half, dst in enumerate((up_ref, lo_ref)):
                part = full[half * TOK : (half + 1) * TOK]
                if rimmed and w == CHUNK - 1:
                    pad = jnp.zeros((8, D), f32)
                    dst[at, w * TOK :] = jnp.concatenate([part[:RIM], pad], axis=0).astype(bf16)
                    edges[half][at] = jnp.concatenate([part[RIM:], pad], axis=0).astype(bf16)
                else:
                    dst[at, w * TOK : (w + 1) * TOK] = part.astype(bf16)


def behind_kernel(
    x_ref, g_ref, upa_ref, loa_ref, upb_ref, lob_ref, eup_ref, elo_ref, place_ref, cut_ref,
    o_ref, gf_ref,
):
    def finish(a_ref, b_ref, e_ref):
        both = []
        for at in range(2):
            both.append(
                mm(place_ref[:, :SPLIT], a_ref[at])
                + mm(place_ref[:, SPLIT:], b_ref[at])
                + mm(cut_ref[...], e_ref[at])
            )
        branch, gn = both
        x = x_ref[...].reshape(HALF, D).astype(f32)
        c = x - jnp.mean(x, axis=-1, keepdims=True)
        rstd = lax.rsqrt(jnp.mean(c * c, axis=-1, keepdims=True) + 1e-5)
        xhat = c * rstd
        o_ref[...] = (x + branch).astype(bf16).reshape(LEV, SHIFT, COLS, D)
        along = jnp.mean(gn * xhat, axis=-1, keepdims=True)
        dx = rstd * (gn - jnp.mean(gn, axis=-1, keepdims=True) - xhat * along)
        g = g_ref[...].reshape(HALF, D).astype(f32)
        gf_ref[...] = (g + dx).astype(bf16).reshape(LEV, SHIFT, COLS, D)

    @pl.when(pl.program_id(0) == 0)
    def _():
        finish(loa_ref, lob_ref, elo_ref)

    @pl.when(pl.program_id(0) == 1)
    def _():
        finish(upa_ref, upb_ref, eup_ref)


def sum_kernel(parts_ref, by_ref, o_ref):
    total = parts_ref[0].astype(f32)
    for i in range(1, LONS // 2):
        total = total + parts_ref[i].astype(f32)
    o_ref[...] = move(by_ref[...], total.astype(bf16)).reshape(LATS, 8, D)


def last_kernel(parts_ref, qkv_ref, out_ref):
    total = parts_ref[0].astype(f32)
    for i in range(1, LATS):
        total = total + parts_ref[i].astype(f32)
    qkv_ref[...] = total[:SPAN]
    out_ref[...] = total[SPAN:]


def send(x, place):
    pairs = []
    for i in range(LATS):
        for j in range(LONS):
            lat, lon = place(i, j)
            pairs.append((i * LONS + j, lat % LATS * LONS + lon % LONS))
    return lax.ppermute(x, ("lat", "lon"), pairs)


def unsend(x, place):
    pairs = []
    for i in range(LATS):
        for j in range(LONS):
            lat, lon = place(i, j)
            pairs.append((lat % LATS * LONS + lon % LONS, i * LONS + j))
    return lax.ppermute(x, ("lat", "lon"), pairs)


def to_upper(i, j):
    return i ^ 1, j


def to_lower(i, j):
    return (i, j) if i % 2 else (i - 2, j)


def to_upper_rim(i, j):
    return i ^ 1, j - 1


def to_lower_rim(i, j):
    return (i, j - 1) if i % 2 else (i - 2, j - 1)


def shaped(*shape, dtype=bf16):
    return jax.ShapeDtypeStruct(shape, dtype)


def call(kernel, us, vmem=VMEM, **kwargs):
    cost = pl.CostEstimate(flops=int(us * 1e9), bytes_accessed=1024, transcendentals=0)
    params = pltpu.CompilerParams(vmem_limit_bytes=vmem)
    return pl.pallas_call(kernel, cost_estimate=cost, compiler_params=params, **kwargs)


def whole(shape):
    return pl.BlockSpec(shape, lambda *_: (0,) * len(shape))


def fixed(shape):
    return pl.BlockSpec(shape, lambda *_: (0,) * len(shape), pipeline_mode=pl.Buffered(1))


def anywhere(count):
    return [pl.BlockSpec(memory_space=pl.ANY)] * count


def scratches():
    stack = HPG * WTOK
    return [
        *[pltpu.VMEM((CTOK, QUAD), bf16)] * 2,
        *[pltpu.VMEM((CHUNK, WTOK, stack), f32)] * 2,
        *[pltpu.VMEM((CHUNK, WTOK, stack), bf16)] * 2,
        *[pltpu.VMEM((CHUNK, stack, QUAD), bf16)] * 2,
    ]


def common():
    return [
        pltpu.VMEM((CTOK, D), bf16),
        pltpu.VMEM((CTOK, D), bf16),
        pltpu.VMEM((FLAGS, D), bf16),
        pltpu.VMEM((D, 3 * D), bf16),
        pltpu.VMEM((D, D), bf16),
        pltpu.VMEM((GROUPS, CTOK, QUAD), bf16),
        pltpu.VMEM((GROUPS, CTOK, 3 * QUAD), bf16),
    ]


ATT, ROWSET = (GROUPS, CTOK, QUAD), (GROUPS, CTOK, 3 * QUAD)


def first_chunk(up, lo, qkv_weight, out_weight):
    ret = (2, SPLIT, D)
    return call(
        chunk_a_kernel,
        13,
        in_specs=anywhere(4),
        out_specs=anywhere(4),
        out_shape=[shaped(*o) for o in (ATT, ROWSET, ret, ret)],
        scratch_shapes=[
            *common(),
            pltpu.VMEM(ret, bf16),
            pltpu.VMEM(ret, bf16),
            pltpu.SemaphoreType.DMA((4 * CHUNK + 3,)),
            pltpu.SemaphoreType.DMA((2 * GROUPS + 2,)),
            *scratches(),
        ],
    )(up, lo, qkv_weight, out_weight)


def second_chunk(core, upa, loa, up, lo, eup, elo, qkv_weight, out_weight, att, rows):
    by_lon, out_by_lon = jnp.asarray(BY_LON, bf16), jnp.asarray(OUT_BY_LON, bf16)
    ready = (LONS // 2, READY, D)
    ret, rim = (2, PACKED - SPLIT, D), (2, RIMP, D)
    return call(
        chunk_b_kernel,
        18,
        in_specs=[pl.BlockSpec(memory_space=pltpu.SMEM)] + anywhere(12),
        out_specs=anywhere(6),
        out_shape=[shaped(*o) for o in (ready, ready, ret, ret, rim, rim)],
        scratch_shapes=[
            *common(),
            pltpu.SemaphoreType.DMA((4 * (CHUNK - 1) + 7,)),
            pltpu.SemaphoreType.DMA((6,)),
            pltpu.SemaphoreType.DMA((4 * CHUNK + 4,)),
            pltpu.VMEM((2, 2, RIMP, D), bf16),
            pltpu.VMEM((2, 2, RIMP, D), bf16),
            pltpu.VMEM((CTOK, D), bf16),
            pltpu.VMEM((CTOK, D), bf16),
            pltpu.VMEM(ATT, bf16),
            pltpu.VMEM(ROWSET, bf16),
            pltpu.VMEM(by_lon.shape[1:], bf16),
            pltpu.VMEM(out_by_lon.shape[1:], bf16),
            pltpu.VMEM((2, *ready), bf16),
            pltpu.VMEM(ret, bf16),
            pltpu.VMEM(ret, bf16),
            pltpu.VMEM(rim, bf16),
            pltpu.VMEM(rim, bf16),
            *scratches(),
        ],
    )(core, upa, loa, up, lo, eup, elo, qkv_weight, out_weight, att, rows, by_lon, out_by_lon)


def groups_of(*keys):
    groups = {}
    for i in range(LATS):
        for j in range(LONS):
            parts = split(i, j)
            groups.setdefault(tuple(parts[k] for k in keys), []).append(i * LONS + j)
    return list(groups.values())


def other_core(i, j):
    return i, j ^ 1


def shards(features, regions, qkv_weight, out_weight, grad_output):
    place, cut = jnp.asarray(PLACE, bf16), jnp.asarray(CUT, bf16)
    core = (lax.axis_index("lon") % 2).reshape(1)
    a, b, edge = (2, SPLIT, D), (2, PACKED - SPLIT, D), (2, RIMP, D)
    early = pl.BlockSpec((LEV, ROWS, EARLY, D), lambda i: (0, 0, 0, 0))
    up_shape = (2, SPLIT + FLAGS, D)
    upa, loa = call(
        early_kernel,
        3,
        grid=(1,),
        in_specs=[early, early, whole(regions.shape), whole(EARLY_PLACE.shape)],
        out_specs=[whole(up_shape), whole(a)],
        out_shape=[shaped(*up_shape), shaped(*a)],
        scratch_shapes=[pltpu.VMEM((LEV, ROWS, EARLY, D), bf16)],
    )(features, grad_output, regions, jnp.asarray(EARLY_PLACE, bf16))
    features, grad_output, upa, loa = lax.optimization_barrier((features, grad_output, upa, loa))
    upa, loa = send(upa, to_upper), send(loa, to_lower)
    upb, lob, eup, elo = call(
        late_kernel,
        5,
        out_shape=[shaped(*s) for s in (b, b, edge, edge)],
        scratch_shapes=[pltpu.VMEM((LEV, ROWS, COLS, D), bf16)],
    )(features, grad_output, jnp.asarray(LATE_PLACE, bf16), cut)
    upb, lob = send(upb, to_upper), send(lob, to_lower)
    eup, elo = send(eup, to_upper_rim), send(elo, to_lower_rim)
    weights = (qkv_weight, out_weight)

    atta, rowsa, rupa, rloa = first_chunk(upa, loa, *weights)
    atta, rupa, rloa = lax.optimization_barrier((atta, rupa, rloa))
    rupa, rloa = unsend(rupa, to_upper), unsend(rloa, to_lower)
    mine, theirs, rupb, rlob, reup, relo = second_chunk(
        core, upa, loa, upb, lob, eup, elo, *weights, atta, rowsa
    )
    rupb, theirs, rupa, rloa = lax.optimization_barrier((rupb, theirs, rupa, rloa))
    theirs = send(theirs, other_core)
    theirs, rupb, rlob = lax.optimization_barrier((theirs, rupb, rlob))
    ready = (mine.astype(f32) + theirs.astype(f32)).astype(bf16)
    parts = lax.all_to_all(ready, ("lat", "lon"), 0, 0, axis_index_groups=groups_of(0, 2))
    rupb, rlob = unsend(rupb, to_upper), unsend(rlob, to_lower)
    reup, relo = unsend(reup, to_upper_rim), unsend(relo, to_lower_rim)
    half = pl.BlockSpec((LEV, SHIFT, COLS, D), lambda i: (0, i, 0, 0))
    returned = (rupa, rloa, rupb, rlob, reup, relo, place.T, cut.T)
    output, grad_features = call(
        behind_kernel,
        6,
        MOST,
        grid=(2,),
        in_specs=[half, half] + [fixed(r.shape) for r in returned],
        out_specs=[half, half],
        out_shape=[shaped(*features.shape)] * 2,
    )(features, grad_output, *returned)

    lat, lon = lax.axis_index("lat"), lax.axis_index("lon")
    by_lat = jnp.asarray(BY_LAT, bf16)[lon % 2 * LONS // 2 + lat // 2 % 2 * 4 + lon // 4]
    part = call(sum_kernel, 2, MOST, out_shape=shaped(LATS, 8, D))(parts, by_lat)
    part = lax.all_to_all(part, ("lat", "lon"), 0, 0, axis_index_groups=groups_of(0, 1))
    grad_qkv, grad_out = call(
        last_kernel,
        1,
        MOST,
        out_shape=[shaped(SPAN, D, dtype=f32), shaped(SPAN_OUT, D, dtype=f32)],
    )(part)
    return (output, grad_features, grad_qkv.T, grad_out.T)


def solution(mesh):
    return jax.shard_map(
        shards,
        mesh=mesh,
        in_specs=(
            P(None, "lat", "lon", None),
            P("lat", "lon"),
            P(),
            P(),
            P(None, "lat", "lon", None),
        ),
        out_specs=(
            P(None, "lat", "lon", None),
            P(None, "lat", "lon", None),
            P(None, ("lat", "lon")),
            P(None, ("lat", "lon")),
        ),
        check_vma=False,
    )
```

```python
import functools

import jax
import jax.numpy as jnp
import numpy as np
from jax import lax
from jax.experimental import pallas as pl
from jax.experimental.pallas import tpu as pltpu
from jax.sharding import PartitionSpec as P

HEADS = 8
WINDOW = 12
SHIFT = 6
LEV, ROWS, COLS, D = 2, 12, 48, 512
LATS, LONS = 16, 16
HALF = LEV * SHIFT * COLS
WINS = COLS // WINDOW
TOK = HALF // WINS
WTOK = 2 * TOK
RIM = LEV * SHIFT * SHIFT
RIMP = 80
PACKED = HALF - RIM + 8
QUAD = 256
GROUPS = D // QUAD
HPG = 4
HD = 64
CHUNK = 2
CTOK = CHUNK * WTOK
SPLIT = CHUNK * TOK
LOG2E = 1.4426950408889634
VMEM = 60 * 1024 * 1024
LESS = 48 * 1024 * 1024
MOST = 63 * 1024 * 1024 + 512 * 1024
NT = (((1,), (1,)), ((), ()))
TN = (((0,), (0,)), ((), ()))
f32, bf16 = jnp.float32, jnp.bfloat16
SPAN = 3 * D // (LATS * LONS)
SPAN_OUT = D // (LATS * LONS)
CLASSES = 4
PLACES = LATS * LONS // (2 * CLASSES)
GW = 3 * QUAD // (2 * CLASSES)
GO = SPAN_OUT * PLACES
READY = GROUPS * GW + GO
FLAGS = 16


EARLY = 32


def one_hots():
    early = np.zeros((SPLIT, LEV * SHIFT * EARLY), np.float32)
    late = np.zeros((PACKED - SPLIT, HALF), np.float32)
    place = np.zeros((PACKED, HALF), np.float32)
    cut = np.zeros((RIMP, HALF), np.float32)
    for line in range(LEV * SHIFT):
        for col in range(COLS - SHIFT):
            win, at = divmod(col, WINDOW)
            wide = WINDOW if win < WINS - 1 else SHIFT
            to = win * TOK + line * wide + at
            place[to, line * COLS + col + SHIFT] = 1
            if win < CHUNK:
                early[to, line * EARLY + col + SHIFT] = 1
            else:
                late[to - SPLIT, line * COLS + col + SHIFT] = 1
        for col in range(SHIFT):
            cut[line * SHIFT + col, line * COLS + col] = 1
    return early, late, place, cut


def split(lat, lon):
    return lon % 2, lon // 4, lat * 2 + lon // 2 % 2


def orders():
    by_class = np.zeros((2, GROUPS, 2 * CLASSES * GW, 3 * QUAD), np.float32)
    out_by_class = np.zeros((2, D, D), np.float32)
    by_place = np.zeros((2 * CLASSES, PLACES * 8, PLACES * 8), np.float32)
    for group in range(GROUPS):
        filled = np.zeros((2, CLASSES), np.int64)
        for row in range(3 * QUAD):
            column = row // QUAD * D + group * QUAD + row % QUAD
            device, at = divmod(column, SPAN)
            core, rest, within = split(*divmod(device, LONS))
            slot = filled[core, rest]
            for mine in range(2):
                to = ((core ^ mine) * CLASSES + rest) * GW + slot
                by_class[mine, group, to, row] = 1
            by_place[core * CLASSES + rest, within * 8 + at, group * GW + slot] = 1
            filled[core, rest] += 1
        assert (filled == GW).all()
    for row in range(D):
        device, at = divmod(row, SPAN_OUT)
        core, rest, within = split(*divmod(device, LONS))
        slot = within * SPAN_OUT + at
        for mine in range(2):
            out_by_class[mine, ((core ^ mine) * CLASSES + rest) * GO + slot, row] = 1
        by_place[core * CLASSES + rest, within * 8 + SPAN + at, GROUPS * GW + slot] = 1
    return by_class, out_by_class, by_place


EARLY_PLACE, LATE_PLACE, PLACE, CUT = one_hots()
BY_LON, OUT_BY_LON, BY_LAT = orders()


def mm(a, b, dims=(((1,), (0,)), ((), ()))):
    return lax.dot_general(a, b, dims, preferred_element_type=f32)


def move(one_hot, x):
    return mm(one_hot, x).astype(bf16)


def normalize(x):
    c = x - jnp.mean(x, axis=-1, keepdims=True)
    return c * lax.rsqrt(jnp.mean(c * c, axis=-1, keepdims=True) + 1e-5)


def early_kernel(x_ref, g_ref, regions_ref, place_ref, up_ref, lo_ref, n_s):
    for lev in range(LEV):
        x = x_ref[lev].reshape(ROWS * EARLY, D).astype(f32)
        n_s[lev] = normalize(x).astype(bf16).reshape(ROWS, EARLY, D)
    for at, src in enumerate((n_s, g_ref)):
        lower = src[:, :SHIFT].reshape(LEV * SHIFT * EARLY, D)
        upper = src[:, SHIFT:].reshape(LEV * SHIFT * EARLY, D)
        up_ref[at, :SPLIT] = move(place_ref[...], upper)
        lo_ref[at] = move(place_ref[...], lower)
        up_ref[at, SPLIT:] = jnp.zeros((FLAGS, D), bf16)
    same = jnp.where(regions_ref[0:1] == regions_ref[SHIFT : SHIFT + 1], 1.0, 0.0)
    row = lax.broadcasted_iota(jnp.int32, (COLS, D), 0)
    lane = lax.broadcasted_iota(jnp.int32, (COLS, D), 1)
    spread = jnp.where(row == lane, 1.0, 0.0).astype(bf16)
    up_ref[0, SPLIT:] = move(jnp.broadcast_to(same, (FLAGS, COLS)).astype(bf16), spread)


def late_kernel(x_ref, g_ref, place_ref, cut_ref, up_ref, lo_ref, eup_ref, elo_ref, n_s):
    for lev in range(LEV):
        x = x_ref[lev].reshape(ROWS * COLS, D).astype(f32)
        n_s[lev] = normalize(x).astype(bf16).reshape(ROWS, COLS, D)
    for at, src in enumerate((n_s, g_ref)):
        for rows, dst, rim in (
            (slice(SHIFT, ROWS), up_ref, eup_ref),
            (slice(0, SHIFT), lo_ref, elo_ref),
        ):
            half = src[:, rows].reshape(HALF, D)
            dst[at] = move(place_ref[...], half)
            rim[at] = move(cut_ref[...], half)


def attend(flags, first, group, x_s, g_s, wqkv_s, wout_s, att_s, rows_s, scratch):
    k_s, v_s, s_s, dp_s, p_s, ds_s, qs_s, gs_s = scratch
    lane = lax.broadcasted_iota(jnp.int32, (1, QUAD), 1)
    head_of = lane // HD
    at = group * QUAD
    wq, wk, wv = (wqkv_s[:, D * i + at : D * i + at + QUAD] for i in range(3))
    wo = wout_s[at : at + QUAD]
    query = lax.broadcasted_iota(jnp.int32, (1, HPG * WTOK), 1)
    in_upper = lax.rem(query, WTOK) < TOK

    def project(w):
        rows = slice(w * WTOK, (w + 1) * WTOK)
        x = x_s[rows]
        k_s[rows] = mm(x, wk).astype(bf16)
        v_s[rows] = mm(x, wv).astype(bf16)
        q = mm(x, wq).astype(bf16)
        a = mm(g_s[rows], wo, NT).astype(bf16)
        for h in range(HPG):
            qs_s[w, h * WTOK : (h + 1) * WTOK] = jnp.where(head_of == h, q, jnp.zeros_like(q))
            gs_s[w, h * WTOK : (h + 1) * WTOK] = jnp.where(head_of == h, a, jnp.zeros_like(a))

    def score(w, cols):
        rows = slice(w * WTOK, (w + 1) * WTOK)
        s_s[w, :, cols] = mm(k_s[rows], qs_s[w, cols], NT)
        dp_s[w, :, cols] = mm(v_s[rows], gs_s[w, cols], NT)

    def soften(w, cols):
        here = lax.broadcasted_iota(jnp.int32, (1, D), 1) == WINDOW * (first + w)
        flag = jnp.sum(jnp.where(here, flags, 0.0), axis=1, keepdims=True)
        same = jnp.broadcast_to(flag, (1, 128)) > 0.5
        up = in_upper[:, cols]
        s_up, s_lo = s_s[w, :TOK, cols], s_s[w, TOK:, cols]
        m_up = jnp.max(s_up, axis=0, keepdims=True)
        m_lo = jnp.max(s_lo, axis=0, keepdims=True)
        m = jnp.where(same, jnp.maximum(m_up, m_lo), jnp.where(up, m_up, m_lo))
        from_up = jnp.where(jnp.logical_or(same, up), m, 1e30)
        from_lo = jnp.where(jnp.logical_and(jnp.logical_not(same), up), 1e30, m)
        c = LOG2E * HD**-0.5
        e_up = jnp.exp2((s_up - from_up) * c)
        e_lo = jnp.exp2((s_lo - from_lo) * c)
        total = jnp.sum(e_up, axis=0, keepdims=True) + jnp.sum(e_lo, axis=0, keepdims=True)
        p = jnp.concatenate([e_up, e_lo], axis=0) * (1.0 / total)
        p_s[w, :, cols] = p.astype(bf16)
        dp = dp_s[w, :, cols]
        delta = jnp.sum(dp * p, axis=0, keepdims=True)
        ds_s[w, :, cols] = (p * ((dp - delta) * HD**-0.5)).astype(bf16)

    def pick(stack):
        out = stack[:WTOK]
        for h in range(1, HPG):
            out = jnp.where(head_of == h, stack[h * WTOK : (h + 1) * WTOK], out)
        return out.astype(bf16)

    def finish(w, part):
        rows = slice(w * WTOK, (w + 1) * WTOK)
        if part == 0:
            att_s[group, rows] = pick(mm(p_s[w], v_s[rows], TN))
        elif part == 1:
            rows_s[group, rows, 0:256] = pick(mm(ds_s[w], k_s[rows], TN))
        elif part == 2:
            rows_s[group, rows, 256:512] = mm(ds_s[w], qs_s[w]).astype(bf16)
        else:
            rows_s[group, rows, 512:768] = mm(p_s[w], gs_s[w]).astype(bf16)

    wide = HPG * WTOK
    tiles = [slice(i, min(i + 256, wide)) for i in range(0, wide, 256)]
    for t in range(CHUNK):
        project(t)
        for tile in tiles:
            score(t, tile)
            for i in range(tile.start, tile.stop, 128):
                soften(t, slice(i, i + 128))
        for j in range(4):
            finish(t, j)


def starts(pairs, sems):
    copies = [pltpu.make_async_copy(src, dst, sems.at[i]) for i, (src, dst) in enumerate(pairs)]
    for copy in copies:
        copy.start()
    return copies


def waits(copies):
    for copy in copies:
        copy.wait()


def whole_windows(up, lo, at, dst, count):
    pairs = []
    for w in range(count):
        for half, src in enumerate((up, lo)):
            to = w * WTOK + half * TOK
            pairs.append((src.at[at, pl.ds(w * TOK, TOK)], dst.at[pl.ds(to, TOK)]))
    return pairs


def chunk_a_kernel(up, lo, wqkv, wout, att, rows, rup, rlo, *refs):
    x_s, g_s, flag_s, wqkv_s, wout_s, att_s, rows_s, rup_s, rlo_s, in_sems, out_sems = refs[:11]
    scratch = refs[11:]
    copies = starts(
        [
            *whole_windows(up, lo, 0, x_s, CHUNK),
            (wqkv, wqkv_s),
            (up.at[0, pl.ds(SPLIT, FLAGS)], flag_s),
            *whole_windows(up, lo, 1, g_s, CHUNK),
            (wout, wout_s),
        ],
        in_sems,
    )
    waits(copies)
    flags = flag_s[...].astype(f32)[0:1]
    outs = []
    for group in range(GROUPS):
        attend(flags, 0, group, x_s, g_s, wqkv_s, wout_s, att_s, rows_s, scratch)
        pairs = [(att_s.at[group], att.at[group]), (rows_s.at[group], rows.at[group])]
        outs += starts(pairs, out_sems.at[pl.ds(2 * group, 2)])
    back(False, att_s, rows_s, wqkv_s, wout_s, rup_s, rlo_s)
    outs += starts([(rup_s, rup), (rlo_s, rlo)], out_sems.at[pl.ds(2 * GROUPS, 2)])
    waits(outs)


def chunk_b_kernel(
    core_ref, upa, loa, up, lo, eup, elo, wqkv, wout, atta, rowsa, by_lon, out_by_lon,
    mine, theirs, rup, rlo, reup, relo, *refs,
):
    x_s, g_s, flag_s, wqkv_s, wout_s, att_s, rows_s, in_sems, out_sems, late_sems = refs[:10]
    here_s, there_s, xa_s, ga_s, atta_s, rowsa_s, by_s, out_by_s, o_s, rup_s, rlo_s, reup_s, relo_s = refs[10:23]
    scratch = refs[23:]
    core = core_ref[0]
    last = pl.ds((CHUNK - 1) * TOK, RIMP)
    copies = starts(
        [
            *whole_windows(up, lo, 0, x_s, CHUNK - 1),
            *whole_windows(up, lo, 1, g_s, CHUNK - 1),
            (up.at[:, last], here_s.at[0]),
            (lo.at[:, last], here_s.at[1]),
            (eup, there_s.at[0]),
            (elo, there_s.at[1]),
            (wqkv, wqkv_s),
            (wout, wout_s),
            (upa.at[0, pl.ds(SPLIT, FLAGS)], flag_s),
        ],
        in_sems,
    )
    late = starts(
        [
            *whole_windows(upa, loa, 0, xa_s, CHUNK),
            *whole_windows(upa, loa, 1, ga_s, CHUNK),
            (atta, atta_s),
            (rowsa, rowsa_s),
            (by_lon.at[core], by_s),
            (out_by_lon.at[core], out_by_s),
        ],
        late_sems,
    )
    waits(copies)
    for at, dst in enumerate((x_s, g_s)):
        for half in range(2):
            here = here_s[half, at].astype(f32)[:RIM]
            there = there_s[half, at].astype(f32)[:RIM]
            to = (CHUNK - 1) * WTOK + half * TOK
            dst[to : to + TOK] = jnp.concatenate([here, there], axis=0).astype(bf16)
    flags = flag_s[...].astype(f32)[0:1]
    for group in range(GROUPS):
        attend(flags, CHUNK, group, x_s, g_s, wqkv_s, wout_s, att_s, rows_s, scratch)
        if group == 0:
            waits(late)
        total = mm(xa_s[...], rowsa_s[group], TN) + mm(x_s[...], rows_s[group], TN)
        ready = mm(by_s[group], total.astype(bf16), NT).astype(bf16)
        o_s[:, :, group * GW : (group + 1) * GW] = ready.reshape(2, CLASSES, GW, D)
        out = (mm(atta_s[group], ga_s[...], TN) + mm(att_s[group], g_s[...], TN)).astype(bf16)
        out = mm(out_by_s[...], out, NT).astype(bf16).reshape(2, CLASSES, GO, QUAD)
        o_s[:, :, GROUPS * GW :, group * QUAD : (group + 1) * QUAD] = out
    outs = starts([(o_s.at[0], mine), (o_s.at[1], theirs)], out_sems.at[pl.ds(0, 2)])
    back(True, att_s, rows_s, wqkv_s, wout_s, rup_s, rlo_s, reup_s, relo_s)
    pairs = [(rup_s, rup), (rlo_s, rlo), (reup_s, reup), (relo_s, relo)]
    outs += starts(pairs, out_sems.at[pl.ds(2, 4)])
    waits(outs)


def back(rimmed, att_s, rows_s, wqkv_s, wout_s, up_ref, lo_ref, *edges):
    for w in range(CHUNK):
        rows = slice(w * WTOK, (w + 1) * WTOK)
        branch = gn = 0.0
        for i in range(GROUPS):
            branch = branch + mm(att_s[i, rows], wout_s[QUAD * i : QUAD * (i + 1)])
            for j in range(3):
                at = D * j + QUAD * i
                gn = gn + mm(rows_s[i, rows, QUAD * j : QUAD * (j + 1)], wqkv_s[:, at : at + QUAD], NT)
        for at, full in enumerate((branch, gn)):
            for half, dst in enumerate((up_ref, lo_ref)):
                part = full[half * TOK : (half + 1) * TOK]
                if rimmed and w == CHUNK - 1:
                    pad = jnp.zeros((8, D), f32)
                    dst[at, w * TOK :] = jnp.concatenate([part[:RIM], pad], axis=0).astype(bf16)
                    edges[half][at] = jnp.concatenate([part[RIM:], pad], axis=0).astype(bf16)
                else:
                    dst[at, w * TOK : (w + 1) * TOK] = part.astype(bf16)


def behind_kernel(
    x_ref, g_ref, upa_ref, loa_ref, upb_ref, lob_ref, eup_ref, elo_ref, place_ref, cut_ref,
    o_ref, gf_ref,
):
    def finish(a_ref, b_ref, e_ref):
        both = []
        for at in range(2):
            both.append(
                mm(place_ref[:, :SPLIT], a_ref[at])
                + mm(place_ref[:, SPLIT:], b_ref[at])
                + mm(cut_ref[...], e_ref[at])
            )
        branch, gn = both
        x = x_ref[...].reshape(HALF, D).astype(f32)
        c = x - jnp.mean(x, axis=-1, keepdims=True)
        rstd = lax.rsqrt(jnp.mean(c * c, axis=-1, keepdims=True) + 1e-5)
        xhat = c * rstd
        o_ref[...] = (x + branch).astype(bf16).reshape(LEV, SHIFT, COLS, D)
        along = jnp.mean(gn * xhat, axis=-1, keepdims=True)
        dx = rstd * (gn - jnp.mean(gn, axis=-1, keepdims=True) - xhat * along)
        g = g_ref[...].reshape(HALF, D).astype(f32)
        gf_ref[...] = (g + dx).astype(bf16).reshape(LEV, SHIFT, COLS, D)

    @pl.when(pl.program_id(0) == 0)
    def _():
        finish(loa_ref, lob_ref, elo_ref)

    @pl.when(pl.program_id(0) == 1)
    def _():
        finish(upa_ref, upb_ref, eup_ref)


def sum_kernel(parts_ref, by_ref, o_ref):
    total = parts_ref[0].astype(f32)
    for i in range(1, CLASSES):
        total = total + parts_ref[i].astype(f32)
    o_ref[...] = move(by_ref[...], total.astype(bf16)).reshape(PLACES, 8, D)


def last_kernel(parts_ref, qkv_ref, out_ref):
    total = parts_ref[0].astype(f32)
    for i in range(1, PLACES):
        total = total + parts_ref[i].astype(f32)
    qkv_ref[...] = total[:SPAN]
    out_ref[...] = total[SPAN:]


def send(x, place):
    pairs = []
    for i in range(LATS):
        for j in range(LONS):
            lat, lon = place(i, j)
            pairs.append((i * LONS + j, lat % LATS * LONS + lon % LONS))
    return lax.ppermute(x, ("lat", "lon"), pairs)


def unsend(x, place):
    pairs = []
    for i in range(LATS):
        for j in range(LONS):
            lat, lon = place(i, j)
            pairs.append((lat % LATS * LONS + lon % LONS, i * LONS + j))
    return lax.ppermute(x, ("lat", "lon"), pairs)


def to_upper(i, j):
    return i ^ 1, j


def to_lower(i, j):
    return (i, j) if i % 2 else (i - 2, j)


def to_upper_rim(i, j):
    return i ^ 1, j - 1


def to_lower_rim(i, j):
    return (i, j - 1) if i % 2 else (i - 2, j - 1)


def shaped(*shape, dtype=bf16):
    return jax.ShapeDtypeStruct(shape, dtype)


def call(kernel, us, vmem=VMEM, **kwargs):
    cost = pl.CostEstimate(flops=int(us * 1e9), bytes_accessed=1024, transcendentals=0)
    params = pltpu.CompilerParams(vmem_limit_bytes=vmem)
    return pl.pallas_call(kernel, cost_estimate=cost, compiler_params=params, **kwargs)


def whole(shape):
    return pl.BlockSpec(shape, lambda *_: (0,) * len(shape))


def fixed(shape):
    return pl.BlockSpec(shape, lambda *_: (0,) * len(shape), pipeline_mode=pl.Buffered(1))


def anywhere(count):
    return [pl.BlockSpec(memory_space=pl.ANY)] * count


def scratches():
    stack = HPG * WTOK
    return [
        *[pltpu.VMEM((CTOK, QUAD), bf16)] * 2,
        *[pltpu.VMEM((CHUNK, WTOK, stack), f32)] * 2,
        *[pltpu.VMEM((CHUNK, WTOK, stack), bf16)] * 2,
        *[pltpu.VMEM((CHUNK, stack, QUAD), bf16)] * 2,
    ]


def common():
    return [
        pltpu.VMEM((CTOK, D), bf16),
        pltpu.VMEM((CTOK, D), bf16),
        pltpu.VMEM((FLAGS, D), bf16),
        pltpu.VMEM((D, 3 * D), bf16),
        pltpu.VMEM((D, D), bf16),
        pltpu.VMEM((GROUPS, CTOK, QUAD), bf16),
        pltpu.VMEM((GROUPS, CTOK, 3 * QUAD), bf16),
    ]


ATT, ROWSET = (GROUPS, CTOK, QUAD), (GROUPS, CTOK, 3 * QUAD)


def first_chunk(up, lo, qkv_weight, out_weight):
    ret = (2, SPLIT, D)
    return call(
        chunk_a_kernel,
        13,
        in_specs=anywhere(4),
        out_specs=anywhere(4),
        out_shape=[shaped(*o) for o in (ATT, ROWSET, ret, ret)],
        scratch_shapes=[
            *common(),
            pltpu.VMEM(ret, bf16),
            pltpu.VMEM(ret, bf16),
            pltpu.SemaphoreType.DMA((4 * CHUNK + 3,)),
            pltpu.SemaphoreType.DMA((2 * GROUPS + 2,)),
            *scratches(),
        ],
    )(up, lo, qkv_weight, out_weight)


def second_chunk(core, upa, loa, up, lo, eup, elo, qkv_weight, out_weight, att, rows):
    by_lon, out_by_lon = jnp.asarray(BY_LON, bf16), jnp.asarray(OUT_BY_LON, bf16)
    ready = (CLASSES, READY, D)
    ret, rim = (2, PACKED - SPLIT, D), (2, RIMP, D)
    return call(
        chunk_b_kernel,
        18,
        LESS,
        in_specs=[pl.BlockSpec(memory_space=pltpu.SMEM)] + anywhere(12),
        out_specs=anywhere(6),
        out_shape=[shaped(*o) for o in (ready, ready, ret, ret, rim, rim)],
        scratch_shapes=[
            *common(),
            pltpu.SemaphoreType.DMA((4 * (CHUNK - 1) + 7,)),
            pltpu.SemaphoreType.DMA((6,)),
            pltpu.SemaphoreType.DMA((4 * CHUNK + 4,)),
            pltpu.VMEM((2, 2, RIMP, D), bf16),
            pltpu.VMEM((2, 2, RIMP, D), bf16),
            pltpu.VMEM((CTOK, D), bf16),
            pltpu.VMEM((CTOK, D), bf16),
            pltpu.VMEM(ATT, bf16),
            pltpu.VMEM(ROWSET, bf16),
            pltpu.VMEM(by_lon.shape[1:], bf16),
            pltpu.VMEM(out_by_lon.shape[1:], bf16),
            pltpu.VMEM((2, *ready), bf16),
            pltpu.VMEM(ret, bf16),
            pltpu.VMEM(ret, bf16),
            pltpu.VMEM(rim, bf16),
            pltpu.VMEM(rim, bf16),
            *scratches(),
        ],
    )(core, upa, loa, up, lo, eup, elo, qkv_weight, out_weight, att, rows, by_lon, out_by_lon)


def groups_of(*keys):
    groups = {}
    for i in range(LATS):
        for j in range(LONS):
            parts = split(i, j)
            groups.setdefault(tuple(parts[k] for k in keys), []).append(i * LONS + j)
    return list(groups.values())


def other_core(i, j):
    return i, j ^ 1


def shards(features, regions, qkv_weight, out_weight, grad_output):
    place, cut = jnp.asarray(PLACE, bf16), jnp.asarray(CUT, bf16)
    core = (lax.axis_index("lon") % 2).reshape(1)
    a, b, edge = (2, SPLIT, D), (2, PACKED - SPLIT, D), (2, RIMP, D)
    early = pl.BlockSpec((LEV, ROWS, EARLY, D), lambda i: (0, 0, 0, 0))
    up_shape = (2, SPLIT + FLAGS, D)
    upa, loa = call(
        early_kernel,
        3,
        grid=(1,),
        in_specs=[early, early, whole(regions.shape), whole(EARLY_PLACE.shape)],
        out_specs=[whole(up_shape), whole(a)],
        out_shape=[shaped(*up_shape), shaped(*a)],
        scratch_shapes=[pltpu.VMEM((LEV, ROWS, EARLY, D), bf16)],
    )(features, grad_output, regions, jnp.asarray(EARLY_PLACE, bf16))
    features, grad_output, upa, loa = lax.optimization_barrier((features, grad_output, upa, loa))
    upa, loa = send(upa, to_upper), send(loa, to_lower)
    upb, lob, eup, elo = call(
        late_kernel,
        5,
        out_shape=[shaped(*s) for s in (b, b, edge, edge)],
        scratch_shapes=[pltpu.VMEM((LEV, ROWS, COLS, D), bf16)],
    )(features, grad_output, jnp.asarray(LATE_PLACE, bf16), cut)
    upb, lob = send(upb, to_upper), send(lob, to_lower)
    eup, elo = send(eup, to_upper_rim), send(elo, to_lower_rim)
    weights = (qkv_weight, out_weight)

    atta, rowsa, rupa, rloa = first_chunk(upa, loa, *weights)
    atta, rupa, rloa = lax.optimization_barrier((atta, rupa, rloa))
    rupa, rloa = unsend(rupa, to_upper), unsend(rloa, to_lower)
    mine, theirs, rupb, rlob, reup, relo = second_chunk(
        core, upa, loa, upb, lob, eup, elo, *weights, atta, rowsa
    )
    rupb, theirs, rupa, rloa = lax.optimization_barrier((rupb, theirs, rupa, rloa))
    theirs = send(theirs, other_core)
    theirs, rupb, rlob = lax.optimization_barrier((theirs, rupb, rlob))
    ready = (mine.astype(f32) + theirs.astype(f32)).astype(bf16)
    parts = lax.all_to_all(ready, ("lat", "lon"), 0, 0, axis_index_groups=groups_of(0, 2))
    rupb, rlob = unsend(rupb, to_upper), unsend(rlob, to_lower)
    reup, relo = unsend(reup, to_upper_rim), unsend(relo, to_lower_rim)
    half = pl.BlockSpec((LEV, SHIFT, COLS, D), lambda i: (0, i, 0, 0))
    returned = (rupa, rloa, rupb, rlob, reup, relo, place.T, cut.T)
    output, grad_features = call(
        behind_kernel,
        6,
        MOST,
        grid=(2,),
        in_specs=[half, half] + [fixed(r.shape) for r in returned],
        out_specs=[half, half],
        out_shape=[shaped(*features.shape)] * 2,
    )(features, grad_output, *returned)

    lon = lax.axis_index("lon")
    by_lat = jnp.asarray(BY_LAT, bf16)[lon % 2 * CLASSES + lon // 4]
    part = call(sum_kernel, 2, MOST, out_shape=shaped(PLACES, 8, D))(parts, by_lat)
    part = lax.all_to_all(part, ("lat", "lon"), 0, 0, axis_index_groups=groups_of(0, 1))
    grad_qkv, grad_out = call(
        last_kernel,
        1,
        MOST,
        out_shape=[shaped(SPAN, D, dtype=f32), shaped(SPAN_OUT, D, dtype=f32)],
    )(part)
    return (output, grad_features, grad_qkv.T, grad_out.T)


def solution(mesh):
    return jax.shard_map(
        shards,
        mesh=mesh,
        in_specs=(
            P(None, "lat", "lon", None),
            P("lat", "lon"),
            P(),
            P(),
            P(None, "lat", "lon", None),
        ),
        out_specs=(
            P(None, "lat", "lon", None),
            P(None, "lat", "lon", None),
            P(None, ("lat", "lon")),
            P(None, ("lat", "lon")),
        ),
        check_vma=False,
    )
```
